256 devices in a mesh: ctx: 16 (over y, z_lo, core), head: 16 (over x, z_hi).
Axes of the slice: x: 4, y: 4, z: 8 (z_hi: 4, z_lo: 2; z = z_hi * 2 + z_lo), core: 2. Of those that a mesh axis runs over, the one named last changes fastest.
Arguments:
- queries: bfloat16 [2048, 24576], P('ctx', 'head'), may hold values from -400 to 400
- latent: bfloat16 [2048, 576], P('ctx'), may hold values from -6 to 6
- w_uk: bfloat16 [512, 16384], P(None, 'head'), may hold values from -0.25 to 0.25
- w_uv: bfloat16 [512, 16384], P(None, 'head'), may hold values from -0.25 to 0.25
- grad_out: bfloat16 [2048, 16384], P('ctx', 'head'), may hold values from -6 to 6
- positions: int32 [2048], P('ctx'), may hold values from 0 to 2047, as said below
- tool_result: int32 [2048], P('ctx'), may hold values from 0 to 1
Outputs:
- grad_queries: bfloat16 [2048, 24576], P('ctx', 'head')
- grad_latent: float32 [2048, 576], P('ctx')
- grad_w_uk: float32 [512, 16384], P('ctx', 'head')
- grad_w_uv: float32 [512, 16384], P('ctx', 'head')
The draws below stay inside these ranges and needn't reach their ends.
Inputs may be any that keep to these rules, and one draw needn't show every extreme that they name: Every number from 0 to 2047 appears once; each aligned run of 128 slots holds consecutive positions in increasing order.
All inputs are finite; a program needn't handle non-finite values.
Results may differ from the reference program's by a relative error of at most 0.0064.
Values may be sent and summed in bfloat16 or wider, within the bound.
No kernel may reach another device: no remote copies, remote signals or barrier semaphores. Data moves between devices by JAX's collectives and lax.ppermute only.
A program may use at most 128 MiB of HBM per device.

```python
import jax
import jax.numpy as jnp
from jax import lax

DL = 512
DR = 64
DN = 128
DV = 128
TOK_DEV = 128
HEADS = 128
TOKENS = 2048


def layout(key):
    block_order = jax.random.permutation(jax.random.fold_in(key, 211), TOKENS // TOK_DEV)
    slot_index = jnp.arange(TOKENS, dtype=jnp.int32)
    return (block_order[slot_index // TOK_DEV] * TOK_DEV + slot_index % TOK_DEV).astype(jnp.int32)


def rope_base(key):
    return jnp.clip(jax.random.normal(jax.random.fold_in(key, 101), (TOKENS, DR), jnp.float32), -4.0, 4.0)


def draw_positions(key, part):
    return layout(key)


def draw_tool_result(key, part):
    places = layout(key)
    key = jax.random.fold_in(key, 2)
    run_flags = jax.random.randint(key, (TOKENS // 16 + 1,), 0, 3)
    return (run_flags[places // 16] == 0).astype(jnp.int32)


def draw_latent(key, part):
    base_rows = rope_base(key)
    key = jax.random.fold_in(key, 3)
    nope_part = jnp.clip(jax.random.normal(key, (TOKENS, DL), jnp.float32), -6.0, 6.0)
    rope_part = base_rows
    return jnp.concatenate([nope_part, rope_part], axis=1).astype(jnp.bfloat16)


def draw_queries(key, part):
    key = jax.random.fold_in(key, 4)
    first_key, second_key = jax.random.split(key)
    rope_part = jnp.clip(jax.random.normal(second_key, (TOKENS, HEADS, DR), jnp.float32), -6.0, 6.0)
    nope_part = jnp.clip(jax.random.normal(first_key, (TOKENS, HEADS, DN), jnp.float32), -6.0, 6.0)
    joined = jnp.concatenate([nope_part, rope_part], axis=2)
    return joined.reshape(TOKENS, HEADS * (DN + DR)).astype(jnp.bfloat16)


def levels(key, dims, cuts, low, high):
    factor_of, own = 1.0, jax.random.fold_in(key, 6)
    for axis_at, shards_of in cuts:
        heights = jnp.exp(jax.random.uniform(jax.random.fold_in(own, axis_at), (shards_of,), jnp.float32, low / len(cuts), high / len(cuts)))
        factor_of = factor_of * jnp.repeat(heights, dims[axis_at] // shards_of).reshape([-1 if axis == axis_at else 1 for axis in range(len(dims))])
    return factor_of


def gaussian(key, extent, spread, bound, cuts=(), kind=jnp.bfloat16):
    entries = jax.random.normal(key, extent, jnp.float32) * spread
    if len(cuts) > 0:
        entries = levels(key, extent, cuts, -0.22, 0.18) * entries
    return jnp.clip(entries, min=-bound, max=bound).astype(kind)


def setup_inputs(seed: int = 0) -> dict:
    key_list = jax.random.split(jax.random.key(seed), 8)
    return {
        "queries": draw_queries(jax.random.fold_in(key_list[7], 71), 0),
        "latent": draw_latent(jax.random.fold_in(key_list[7], 71), 0),
        "w_uk": gaussian(key_list[2], (DL, HEADS * DN), DL ** -0.5, 0.25, ((1, 16),)),
        "w_uv": gaussian(key_list[3], (DL, HEADS * DV), DL ** -0.5, 0.25, ((1, 16),)),
        "grad_out": gaussian(key_list[4], (TOKENS, HEADS * DV), 1.0, 6.0, ((0, 16), (1, 16))),
        "positions": draw_positions(jax.random.fold_in(key_list[7], 71), 0),
        "tool_result": draw_tool_result(jax.random.fold_in(key_list[7], 71), 0),
    }


big_negative = -1.0e30


def reference(queries, latent, w_uk, w_uv, grad_out, positions, tool_result):
    tok_count = queries.shape[0]
    head_count = w_uk.shape[1] // DN
    score_scale = (DN + DR) ** -0.5
    q_three = queries.reshape(tok_count, head_count, DN + DR)
    lat_nope = latent[:, :DL]
    key_rope = latent[:, DL:]
    key_nope = jnp.dot(lat_nope, w_uk, preferred_element_type=jnp.float32).astype(jnp.bfloat16)
    values = jnp.dot(lat_nope, w_uv, preferred_element_type=jnp.float32).astype(jnp.bfloat16)
    keep_rows = (1 - tool_result).astype(jnp.bfloat16)
    cotangent = grad_out * keep_rows[:, None]
    visible = positions[None, :] <= positions[:, None]

    def one_head(pieces):
        q_head, k_head, v_head, g_head = pieces
        scores = jnp.dot(q_head[:, :DN], k_head.T, preferred_element_type=jnp.float32)
        scores = (scores + jnp.dot(q_head[:, DN:], key_rope.T, preferred_element_type=jnp.float32)) * score_scale
        masked = jnp.where(visible, scores, big_negative)
        row_top = jnp.max(masked, axis=1)
        shifted = jnp.where(visible, jnp.exp(scores - row_top[:, None]), 0.0)
        log_total = row_top + jnp.log(jnp.sum(shifted, axis=1))
        softmax_w = jnp.where(visible, jnp.exp(scores - log_total[:, None]), 0.0)
        attended = jnp.dot(softmax_w, v_head.astype(jnp.float32), precision=lax.Precision.HIGHEST)
        row_delta = jnp.sum(g_head.astype(jnp.float32) * attended, axis=1)
        grad_prob = jnp.dot(g_head, v_head.T, preferred_element_type=jnp.float32)
        dscore = (softmax_w * (grad_prob - row_delta[:, None])).astype(jnp.bfloat16)
        grad_q = jnp.concatenate([jnp.dot(dscore, k_head, preferred_element_type=jnp.float32),
                                  jnp.dot(dscore, key_rope, preferred_element_type=jnp.float32)], axis=1)
        grad_q = (grad_q * score_scale).astype(jnp.bfloat16)
        key_grad = jnp.dot(dscore.T, q_head[:, :DN], preferred_element_type=jnp.float32) * score_scale
        rope_grad = jnp.dot(dscore.T, q_head[:, DN:], preferred_element_type=jnp.float32) * score_scale
        value_grad = jnp.dot(softmax_w.astype(jnp.bfloat16).T, g_head, preferred_element_type=jnp.float32)
        return grad_q, key_grad, rope_grad, value_grad

    stacked = (q_three.transpose(1, 0, 2),
               key_nope.reshape(tok_count, head_count, DN).transpose(1, 0, 2),
               values.reshape(tok_count, head_count, DV).transpose(1, 0, 2),
               cotangent.reshape(tok_count, head_count, DV).transpose(1, 0, 2))
    grad_q, key_grad, rope_grad, value_grad = lax.map(one_head, stacked)
    grad_queries = grad_q.transpose(1, 0, 2).reshape(tok_count, head_count * (DN + DR))
    key_grads = key_grad.transpose(1, 0, 2).reshape(tok_count, head_count * DN)
    value_grads = value_grad.transpose(1, 0, 2).reshape(tok_count, head_count * DV)
    rope_grads = jnp.sum(rope_grad, axis=0)
    grad_nope = jnp.dot(key_grads, w_uk.astype(jnp.float32).T, precision=lax.Precision.HIGHEST)
    grad_nope = grad_nope + jnp.dot(value_grads, w_uv.astype(jnp.float32).T, precision=lax.Precision.HIGHEST)
    grad_latent = jnp.concatenate([grad_nope, rope_grads], axis=1)
    lat_float = lat_nope.astype(jnp.float32)
    grad_w_uk = jnp.dot(lat_float.T, key_grads, precision=lax.Precision.HIGHEST)
    grad_w_uv = jnp.dot(lat_float.T, value_grads, precision=lax.Precision.HIGHEST)
    return (grad_queries, grad_latent, grad_w_uk, grad_w_uv)
```

```python
import functools
import math

import jax
import jax.numpy as jnp
from jax import lax
from jax.experimental import pallas as pl
from jax.experimental.pallas import tpu as pltpu
from jax.sharding import PartitionSpec as P

DL = 512
DR = 64
DN = 128
DV = 128
TOK = 128
HALF = TOK // 2
ROWS = 464
BACK = 320
CHUNK = 512
MASKED = -1e30
BF = jnp.bfloat16
F32 = jnp.float32


def dot(a, b):
    return lax.dot_general(a, b, (((1,), (0,)), ((), ())), preferred_element_type=F32)


def dot_nt(a, b):
    return lax.dot_general(a, b, (((1,), (1,)), ((), ())), preferred_element_type=F32)


def low_lanes(shape):
    return lax.broadcasted_iota(jnp.int32, shape, len(shape) - 1) < DR


def pack_kernel(q_ref, lat_ref, g_ref, pos_ref, tool_ref, out_ref, lat_s, rope_s, keep_s):
    @pl.when(pl.program_id(0) == 0)
    def _():
        lat_s[...] = lat_ref[:DL, :].astype(F32).T.astype(BF)
        rope = jnp.concatenate([jnp.zeros((DR, TOK), F32), lat_ref[DL:, :].astype(F32)], axis=0)
        rope_s[...] = rope.T
        keep = (1 - tool_ref[...]).astype(F32)
        keep_s[...] = jnp.broadcast_to(keep, (TOK, TOK)).T

    low = low_lanes((TOK, TOK))
    rope = rope_s[...]
    mid = pltpu.roll(q_ref[:, 128:256].astype(F32), DR, 1)
    end = pltpu.roll(q_ref[:, 256:384].astype(F32), DR, 1)
    nope = [q_ref[:, 0:128], jnp.where(low, mid, end).astype(BF)]
    ropes = [
        jnp.where(low, q_ref[:, 128:256].astype(F32), rope).astype(BF),
        jnp.where(low, end, rope).astype(BF),
    ]
    order = jnp.broadcast_to((pos_ref[...] // TOK).astype(F32), (16, TOK)).astype(BF)
    for h in range(2):
        cols = slice(h * 128, h * 128 + 128)
        cotangent = (g_ref[:, cols].astype(F32) * keep_s[...]).astype(BF)
        for c in range(2):
            rows = slice(c * HALF, c * HALF + HALF)
            to = 2 * h + c
            for t in range(4):
                out_ref[to, t * HALF : (t + 1) * HALF, :] = lat_s[rows, t * 128 : (t + 1) * 128]
            out_ref[to, 256:320, :] = ropes[h][rows]
            out_ref[to, 320:384, :] = nope[h][rows]
            out_ref[to, 384:448, :] = cotangent[rows]
            out_ref[to, 448:464, :] = order


def pack(queries, lat_t, grad_out, positions, tool_result):
    return pl.pallas_call(
        pack_kernel,
        grid=(4,),
        in_specs=[
            pl.BlockSpec((TOK, 384), lambda i: (0, i)),
            pl.BlockSpec((DL + DR, TOK), lambda i: (0, 0)),
            pl.BlockSpec((TOK, 256), lambda i: (0, i)),
            pl.BlockSpec((1, TOK), lambda i: (0, 0)),
            pl.BlockSpec((1, TOK), lambda i: (0, 0)),
        ],
        out_specs=pl.BlockSpec((4, ROWS, 128), lambda i: (i, 0, 0)),
        out_shape=jax.ShapeDtypeStruct((16, ROWS, 128), BF),
        scratch_shapes=[
            pltpu.VMEM((TOK, DL), BF),
            pltpu.VMEM((TOK, TOK), F32),
            pltpu.VMEM((TOK, TOK), F32),
        ],
        compiler_params=pltpu.CompilerParams(vmem_limit_bytes=60 << 20),
    )(queries, lat_t, grad_out, positions.reshape(1, TOK), tool_result.reshape(1, TOK))


def attend_kernel(ord_ref, own_ref, oth_ref, uk_ref, uv_ref, keep_out, give_out, dq_out, rope_out,
                  lat, met, weights, kv, ts, kt, qs, cs, s_sc, g_sc, ds_sc, kvg, dr, dqs, sems):
    scale = (DN + DR) ** -0.5
    me = lax.axis_index("ctx")
    core = lax.rem(me, 2)
    columns = pl.ds(pl.multiple_of((me // 2) * 128, 128), 128)

    def fetch(src, dst, sem):
        pltpu.make_async_copy(src, dst, sems.at[sem]).start()

    def arrive(ref, sem):
        pltpu.make_async_copy(ref, ref, sems.at[sem]).wait()

    fetch(uk_ref.at[:, columns], weights.at[:, 0:128], 0)
    fetch(uv_ref.at[:, columns], weights.at[:, 128:256], 1)
    for s in range(16):
        fetch(own_ref.at[s, 0:320, :], lat.at[ord_ref[s] * 2 + core], 2)
        fetch(oth_ref.at[s, 0:320, :], lat.at[ord_ref[s] * 2 + 1 - core], 2)
        fetch(own_ref.at[s, 320:448, :], met.at[ord_ref[s]], 3)
    arrive(weights.at[:, 0:128], 0)
    arrive(weights.at[:, 128:256], 1)
    arrive(lat, 2)
    arrive(met, 3)

    low = low_lanes((HALF, TOK))
    for b in range(16):
        rows = slice(b * HALF, (b + 1) * HALF)
        turned = pltpu.roll(lat[2 * b + core, 256:320, :].astype(F32), DR, 1)
        qs[rows, 0:128] = met[b, 0:64, :]
        qs[rows, 128:256] = jnp.where(low, 0.0, turned).astype(BF)
        cs[rows, :] = met[b, 64:128, :]
    for b in range(8):
        rows = slice(b * 256, b * 256 + 256)
        four = range(4 * b, 4 * b + 4)
        tokens = jnp.concatenate(
            [jnp.concatenate([lat[i, t * HALF : (t + 1) * HALF, :] for t in range(4)], axis=1) for i in four], axis=0
        )
        both = dot(tokens, weights[...])
        rope = jnp.concatenate([lat[i, 256:320, :] for i in four], axis=0)
        keys = both[:, 0:128].astype(BF)
        kv[0, rows, :] = keys
        kv[1, rows, :] = both[:, 128:256].astype(BF)
        ts[rows, :] = rope
        kt[0:128, rows] = keys.astype(F32).T.astype(BF)
        kt[128:256, rows] = rope.astype(F32).T.astype(BF)

    factor = scale * math.log2(math.e)
    lane = lax.broadcasted_iota(jnp.int32, (CHUNK, 256), 1)
    qpos = (lane // HALF) * TOK + core * HALF + lax.rem(lane, HALF)
    visible = lax.broadcasted_iota(jnp.int32, (CHUNK, 256), 0) <= qpos
    for p in range(4):
        rows = slice(p * 256, p * 256 + 256)
        chunks = [slice(c * CHUNK, (c + 1) * CHUNK) for c in range(p + 1)]
        top = jnp.full((8, 256), MASKED, F32)
        for c, at in enumerate(chunks):
            s = dot_nt(jnp.concatenate([kv[0, at, :], ts[at, :]], axis=1), qs[rows, :]) * factor
            if c == p:
                s = jnp.where(visible, s, MASKED)
            s_sc[at, :] = s
            g_sc[at, :] = dot_nt(kv[1, at, :], cs[rows, :])
            top = jnp.maximum(top, jnp.max(s.reshape(CHUNK // 8, 8, 256), axis=0))
        top = jnp.max(top, axis=0, keepdims=True)
        total = jnp.zeros((8, 256), F32)
        mixed = jnp.zeros((8, 256), F32)
        for at in chunks:
            e = jnp.exp2(s_sc[at, :] - top)
            s_sc[at, :] = e
            total = total + jnp.sum(e.reshape(CHUNK // 8, 8, 256), axis=0)
            mixed = mixed + jnp.sum((e * g_sc[at, :]).reshape(CHUNK // 8, 8, 256), axis=0)
        share = 1.0 / jnp.sum(total, axis=0, keepdims=True)
        delta = jnp.sum(mixed, axis=0, keepdims=True) * share
        for c, at in enumerate(chunks):
            prob = s_sc[at, :] * share
            ds = (prob * (g_sc[at, :] - delta)).astype(BF)
            ds_sc[at, :] = ds
            key_part = dot(ds, qs[rows, :])
            value_part = dot(prob.astype(BF), cs[rows, :])
            if c == p:
                kvg[0, at, :] = key_part[:, 0:128]
                dr[at, :] = key_part[:, 128:256]
                kvg[1, at, :] = value_part
            else:
                kvg[0, at, :] += key_part[:, 0:128]
                dr[at, :] += key_part[:, 128:256]
                kvg[1, at, :] += value_part
        upto = (p + 1) * CHUNK
        dqs[rows, :] = (dot(kt[:, 0:upto], ds_sc[0:upto, :]) * scale).T

    keep_scale = jnp.where(core == 0, scale, 1.0)
    give_scale = jnp.where(core == 0, 1.0, scale)
    for s in range(16):
        at = pl.ds(pl.multiple_of(ord_ref[s] * TOK, TOK), TOK)
        of = pl.ds(pl.multiple_of(ord_ref[s] * HALF, HALF), HALF)
        keep_out[s, :, :] = (kvg[core, at, :] * keep_scale).astype(BF)
        give_out[s, :, :] = (kvg[1 - core, at, :] * give_scale).astype(BF)
        dq_out[s, :, :] = dqs[of, 0:128].astype(BF)
        rope = dr[at, :] * scale
        turned = pltpu.roll(dqs[of, 128:256], DR, 1)
        rope_out[s, 0:64, :] = jnp.where(low, turned, rope[0:64]).astype(BF)
        rope_out[s, 64:128, :] = rope[64:128].astype(BF)


def attend(orders, own, other, w_uk, w_uv):
    whole = pl.BlockSpec(memory_space=pltpu.VMEM)
    anywhere = pl.BlockSpec(memory_space=pl.ANY)
    return pl.pallas_call(
        attend_kernel,
        in_specs=[pl.BlockSpec(memory_space=pltpu.SMEM), anywhere, anywhere, anywhere, anywhere],
        out_specs=[whole, whole, whole, whole],
        out_shape=[
            jax.ShapeDtypeStruct((16, TOK, 128), BF),
            jax.ShapeDtypeStruct((16, TOK, 128), BF),
            jax.ShapeDtypeStruct((16, HALF, 128), BF),
            jax.ShapeDtypeStruct((16, TOK, 128), BF),
        ],
        scratch_shapes=[
            pltpu.VMEM((32, 320, 128), BF),
            pltpu.VMEM((16, 128, 128), BF),
            pltpu.VMEM((DL, 256), BF),
            pltpu.VMEM((2, 2048, 128), BF),
            pltpu.VMEM((2048, 128), BF),
            pltpu.VMEM((256, 2048), BF),
            pltpu.VMEM((1024, 256), BF),
            pltpu.VMEM((1024, 128), BF),
            pltpu.VMEM((2048, 256), F32),
            pltpu.VMEM((2048, 256), F32),
            pltpu.VMEM((2048, 256), BF),
            pltpu.VMEM((2, 2048, 128), F32),
            pltpu.VMEM((2048, 128), F32),
            pltpu.VMEM((1024, 256), F32),
            pltpu.SemaphoreType.DMA((4,)),
        ],
        compiler_params=pltpu.CompilerParams(vmem_limit_bytes=32 << 20),
    )(orders, own, other, w_uk, w_uv)


def finish_kernel(keep_ref, met_ref, dq_ref, rope_ref, own_ref, oth_ref, out_ref):
    core = lax.rem(lax.axis_index("ctx"), 2)
    total = jnp.zeros((128, DL), F32)
    for i in range(0, 16, 2):
        pair = (keep_ref[i : i + 2].astype(F32) + met_ref[i : i + 2].astype(F32)).astype(BF)
        out_ref[i : i + 2, 0:128, :] = pair
        out_ref[i : i + 2, 128:192, :] = dq_ref[i : i + 2]
        pair = pair.astype(F32).reshape(4, HALF, 128)
        grads = [jnp.where(core == c, pair[j], pair[j + 1]) for c in range(2) for j in (0, 2)]
        grads = jnp.concatenate(grads, axis=0)
        lat = jnp.concatenate(
            [
                jnp.concatenate([ref[j, t * HALF : (t + 1) * HALF, :] for t in range(4)], axis=1)
                for ref in (own_ref, oth_ref)
                for j in (i, i + 1)
            ],
            axis=0,
        )
        total = total + dot(grads.T.astype(BF), lat)
    total = total.T
    turned = pltpu.roll(total, DR, 1)
    low = low_lanes((32, TOK))
    for i in range(16):
        out_ref[i, 192:256, :] = rope_ref[i, 0:64, :]
        for part, first in ((total, 64), (turned, 96)):
            rope = rope_ref[i, first : first + 32, :].astype(F32)
            mine = jnp.where(low, part[i * 32 : i * 32 + 32], rope)
            out_ref[i, 192 + first : 224 + first, :] = mine.astype(BF)


def finish(keep, met, dq, rope, own, other):
    whole = pl.BlockSpec(memory_space=pltpu.VMEM)
    return pl.pallas_call(
        finish_kernel,
        in_specs=[whole] * 6,
        out_specs=whole,
        out_shape=jax.ShapeDtypeStruct((16, BACK, 128), BF),
        compiler_params=pltpu.CompilerParams(vmem_limit_bytes=16 << 20),
    )(keep, met, dq, rope, own, other)


def latent_kernel(r_ref, uk_ref, uv_ref, out_ref):
    keys = jnp.concatenate([r_ref[i, 0:128, :] for i in range(0, 16, 2)], axis=1)
    values = jnp.concatenate([r_ref[i, 0:128, :] for i in range(1, 16, 2)], axis=1)
    out_ref[:DL, :] = (dot_nt(uk_ref[...], keys) + dot_nt(uv_ref[...], values)).astype(BF)
    rope = r_ref[0, 192:320, :].astype(F32)
    for i in range(1, 16):
        rope = rope + r_ref[i, 192:320, :].astype(F32)
    turned = rope.T
    out_ref[DL:, :] = jnp.concatenate([turned[DR:, :], jnp.zeros((DR, TOK), F32)], axis=0).astype(BF)


def latent_terms(received, w_uk, w_uv):
    whole = pl.BlockSpec(memory_space=pltpu.VMEM)
    return pl.pallas_call(
        latent_kernel,
        in_specs=[whole] * 3,
        out_specs=whole,
        out_shape=jax.ShapeDtypeStruct((DL + 2 * DR, TOK), BF),
        compiler_params=pltpu.CompilerParams(vmem_limit_bytes=16 << 20),
    )(received, w_uk, w_uv)


def unpack_kernel(r_ref, q_ref, uk_ref, uv_ref):
    low = low_lanes((HALF, TOK))
    for h in range(0, 8, 2):
        for c in range(2):
            rows = slice(c * HALF, c * HALF + HALF)
            i, j, at = 2 * h + c, 2 * h + 2 + c, h * 192
            q_ref[rows, at : at + 128] = r_ref[i, 128:192, :]
            first = r_ref[i, 192:256, :].astype(F32)
            second = pltpu.roll(r_ref[j, 192:256, :].astype(F32), DR, 1)
            turned = pltpu.roll(r_ref[j, 128:192, :].astype(F32), DR, 1)
            q_ref[rows, at + 128 : at + 256] = jnp.where(low, first, turned).astype(BF)
            q_ref[rows, at + 256 : at + 384] = jnp.where(low, turned, second).astype(BF)
    for i in range(16):
        left = r_ref[i, 256:288, :].astype(F32)
        right = pltpu.roll(r_ref[i, 288:320, :].astype(F32), DR, 1)
        ref = uv_ref if i % 2 else uk_ref
        ref[:, (i // 2) * 128 : (i // 2) * 128 + 128] = jnp.where(low[0:32], left, right)


def unpack(received):
    whole = pl.BlockSpec(memory_space=pltpu.VMEM)
    return pl.pallas_call(
        unpack_kernel,
        in_specs=[whole],
        out_specs=[whole] * 3,
        out_shape=[
            jax.ShapeDtypeStruct((TOK, 1536), BF),
            jax.ShapeDtypeStruct((32, 1024), F32),
            jax.ShapeDtypeStruct((32, 1024), F32),
        ],
        compiler_params=pltpu.CompilerParams(vmem_limit_bytes=16 << 20),
    )(received)


def local(queries, latent, w_uk, w_uv, grad_out, positions, tool_result):
    every = [list(range(16))]
    swap = [(i, i ^ 1) for i in range(16)]

    def exchange(x, axis):
        return lax.all_to_all(x, axis, 0, 0, tiled=True, axis_index_groups=every)

    lat_t = latent.T
    own = exchange(pack(queries, lat_t, grad_out, positions, tool_result), "ctx")
    other = lax.ppermute(own, "ctx", swap)
    orders = own[:, 448, 0].astype(jnp.int32)
    keep, give, dq, rope = attend(orders, own, other, w_uk, w_uv)
    met = lax.ppermute(give, "ctx", swap)
    received = exchange(finish(keep, met, dq, rope, own, other), "ctx")
    terms = latent_terms(received, w_uk, w_uv)
    met_terms = exchange(terms.reshape(16, 40, TOK), "head")
    summed = jnp.sum(met_terms.astype(F32), axis=0).astype(BF)
    spread = exchange(jnp.broadcast_to(summed[None], (16, 40, TOK)), "head")
    grad_latent = spread.reshape(640, TOK)[: DL + DR].astype(F32).T
    grad_queries, grad_w_uk, grad_w_uv = unpack(received)
    return (grad_queries, grad_latent, grad_w_uk, grad_w_uv)


def solution(mesh):
    placed = (
        P("ctx", "head"),
        P("ctx", None),
        P(None, "head"),
        P(None, "head"),
        P("ctx", "head"),
        P("ctx"),
        P("ctx"),
    )
    return jax.shard_map(
        local,
        mesh=mesh,
        in_specs=placed,
        out_specs=(P("ctx", "head"), P("ctx", None), P("ctx", "head"), P("ctx", "head")),
        check_vma=False,
    )
```

```python
import functools
import math

import jax
import jax.numpy as jnp
from jax import lax
from jax.experimental import pallas as pl
from jax.experimental.pallas import tpu as pltpu
from jax.sharding import PartitionSpec as P

DL = 512
DR = 64
DN = 128
DV = 128
TOK = 128
HALF = TOK // 2
ROWS = 464
BACK = 320
PART = (DL + DR) // 4
CHUNK = 512
MASKED = -1e30
BF = jnp.bfloat16
F32 = jnp.float32


def dot(a, b):
    return lax.dot_general(a, b, (((1,), (0,)), ((), ())), preferred_element_type=F32)


def dot_nt(a, b):
    return lax.dot_general(a, b, (((1,), (1,)), ((), ())), preferred_element_type=F32)


def low_lanes(shape):
    return lax.broadcasted_iota(jnp.int32, shape, len(shape) - 1) < DR


def pack_kernel(q_hbm, lat_hbm, g_hbm, pos_hbm, tool_hbm, out_ref, q_ref, lat_ref, g_ref, pos_ref, tool_ref, sems):
    pairs = [(tool_hbm, tool_ref), (pos_hbm, pos_ref), (lat_hbm, lat_ref), (q_hbm, q_ref), (g_hbm, g_ref)]
    copies = [pltpu.make_async_copy(src, dst, sems.at[i]) for i, (src, dst) in enumerate(pairs)]
    for copy in copies:
        copy.start()
    for copy in copies[:3]:
        copy.wait()
    tokens = lat_ref[:DL, :].astype(F32).T.astype(BF)
    rope = jnp.concatenate([jnp.zeros((DR, TOK), F32), lat_ref[DL:, :].astype(F32)], axis=0).T
    keep = jnp.broadcast_to((1 - tool_ref[...]).astype(F32), (TOK, TOK)).T
    order = jnp.broadcast_to((pos_ref[...] // TOK).astype(F32), (16, TOK)).astype(BF)
    halves = [slice(c * HALF, c * HALF + HALF) for c in range(2)]
    for i in range(16):
        for t in range(4):
            out_ref[i, t * HALF : (t + 1) * HALF, :] = tokens[halves[i % 2], t * 128 : (t + 1) * 128]
        out_ref[i, 448:464, :] = order
    for copy in copies[3:]:
        copy.wait()
    low = low_lanes((TOK, TOK))
    for h in range(0, 8, 2):
        at = h * 192
        near = q_ref[:, at + 128 : at + 256].astype(F32)
        mid = pltpu.roll(near, DR, 1)
        end = pltpu.roll(q_ref[:, at + 256 : at + 384].astype(F32), DR, 1)
        nope = [q_ref[:, at : at + 128], jnp.where(low, mid, end).astype(BF)]
        ropes = [jnp.where(low, near, rope).astype(BF), jnp.where(low, end, rope).astype(BF)]
        for k in range(2):
            cotangent = (g_ref[:, (h + k) * 128 : (h + k) * 128 + 128].astype(F32) * keep).astype(BF)
            for c, rows in enumerate(halves):
                to = 2 * (h + k) + c
                out_ref[to, 256:320, :] = ropes[k][rows]
                out_ref[to, 320:384, :] = nope[k][rows]
                out_ref[to, 384:448, :] = cotangent[rows]


def pack(queries, lat_t, grad_out, positions, tool_result):
    return pl.pallas_call(
        pack_kernel,
        in_specs=[pl.BlockSpec(memory_space=pl.ANY)] * 5,
        out_specs=pl.BlockSpec(memory_space=pltpu.VMEM),
        out_shape=jax.ShapeDtypeStruct((16, ROWS, 128), BF),
        scratch_shapes=[
            pltpu.VMEM((TOK, 1536), BF),
            pltpu.VMEM((DL + DR, TOK), BF),
            pltpu.VMEM((TOK, 1024), BF),
            pltpu.VMEM((1, TOK), jnp.int32),
            pltpu.VMEM((1, TOK), jnp.int32),
            pltpu.SemaphoreType.DMA((5,)),
        ],
        compiler_params=pltpu.CompilerParams(vmem_limit_bytes=60 << 20),
    )(queries, lat_t, grad_out, positions.reshape(1, TOK), tool_result.reshape(1, TOK))


def attend_kernel(ord_ref, own_ref, oth_ref, uk_ref, uv_ref, keep_out, give_out, dq_out, rope_out,
                  weights, kv, ts, kt, qs, cs, s_sc, g_sc, ds_sc, kvg, dr, dqs, source, sems):
    scale = (DN + DR) ** -0.5
    me = lax.axis_index("ctx")
    core = lax.rem(me, 2)
    columns = pl.ds(pl.multiple_of((me // 2) * 128, 128), 128)
    copies = [
        pltpu.make_async_copy(ref.at[:, columns], weights.at[:, i * 128 : i * 128 + 128], sems.at[i])
        for i, ref in enumerate((uk_ref, uv_ref))
    ]
    for copy in copies:
        copy.start()
    for s in range(16):
        source[ord_ref[s]] = s

    low = low_lanes((HALF, TOK))
    for b in range(16):
        rows = slice(b * HALF, (b + 1) * HALF)
        turned = pltpu.roll(own_ref[source[b], 256:320, :].astype(F32), DR, 1)
        qs[rows, 0:128] = own_ref[source[b], 320:384, :]
        qs[rows, 128:256] = jnp.where(low, 0.0, turned).astype(BF)
        cs[rows, :] = own_ref[source[b], 384:448, :]
    for copy in copies:
        copy.wait()
    for b in range(8):
        rows = slice(b * 256, b * 256 + 256)
        four = [(ref, source[2 * b + k]) for k in range(2) for ref in (own_ref, oth_ref)]
        tokens = jnp.concatenate(
            [
                jnp.concatenate([ref[i, t * HALF : (t + 1) * HALF, :] for t in range(4)], axis=1)
                for ref, i in four
            ],
            axis=0,
        )
        both = dot(tokens, weights[...])
        rope = jnp.concatenate([ref[i, 256:320, :] for ref, i in four], axis=0)
        keys = both[:, 0:128].astype(BF)
        kv[0, rows, :] = keys
        kv[1, rows, :] = both[:, 128:256].astype(BF)
        ts[rows, :] = rope
        kt[0:128, rows] = keys.astype(F32).T.astype(BF)
        kt[128:256, rows] = rope.astype(F32).T.astype(BF)

    factor = scale * math.log2(math.e)
    lane = lax.broadcasted_iota(jnp.int32, (CHUNK, 256), 1)
    qpos = (lane // HALF) * TOK + core * HALF + lax.rem(lane, HALF)
    row = lax.broadcasted_iota(jnp.int32, (CHUNK, 256), 0)
    kpos = (row // TOK) * TOK + lax.rem(lax.rem(row, TOK) + core * HALF, TOK)
    visible = kpos <= qpos
    for p in range(4):
        rows = slice(p * 256, p * 256 + 256)
        chunks = [slice(c * CHUNK, (c + 1) * CHUNK) for c in range(p + 1)]
        top = jnp.full((8, 256), MASKED, F32)
        for c, at in enumerate(chunks):
            s = dot_nt(jnp.concatenate([kv[0, at, :], ts[at, :]], axis=1), qs[rows, :]) * factor
            if c == p:
                s = jnp.where(visible, s, MASKED)
            s_sc[at, :] = s
            g_sc[at, :] = dot_nt(kv[1, at, :], cs[rows, :])
            top = jnp.maximum(top, jnp.max(s.reshape(CHUNK // 8, 8, 256), axis=0))
        top = jnp.max(top, axis=0, keepdims=True)
        total = jnp.zeros((8, 256), F32)
        mixed = jnp.zeros((8, 256), F32)
        for at in chunks:
            e = jnp.exp2(s_sc[at, :] - top)
            s_sc[at, :] = e
            total = total + jnp.sum(e.reshape(CHUNK // 8, 8, 256), axis=0)
            mixed = mixed + jnp.sum((e * g_sc[at, :]).reshape(CHUNK // 8, 8, 256), axis=0)
        share = 1.0 / jnp.sum(total, axis=0, keepdims=True)
        delta = jnp.sum(mixed, axis=0, keepdims=True) * share
        for c, at in enumerate(chunks):
            prob = s_sc[at, :] * share
            ds = (prob * (g_sc[at, :] - delta)).astype(BF)
            ds_sc[at, :] = ds
            key_part = dot(ds, qs[rows, :])
            value_part = dot(prob.astype(BF), cs[rows, :])
            if c == p:
                kvg[0, at, :] = key_part[:, 0:128]
                dr[at, :] = key_part[:, 128:256]
                kvg[1, at, :] = value_part
            else:
                kvg[0, at, :] += key_part[:, 0:128]
                dr[at, :] += key_part[:, 128:256]
                kvg[1, at, :] += value_part
        upto = (p + 1) * CHUNK
        dqs[rows, :] = (dot(kt[:, 0:upto], ds_sc[0:upto, :]) * scale).T

    keep_scale = jnp.where(core == 0, scale, 1.0)
    give_scale = jnp.where(core == 0, 1.0, scale)
    for s in range(16):
        at = pl.multiple_of(ord_ref[s] * TOK, TOK)
        own_half, oth_half = pl.ds(at, HALF), pl.ds(at + HALF, HALF)
        of = pl.ds(pl.multiple_of(ord_ref[s] * HALF, HALF), HALF)
        keep_out[s, :, :] = (kvg[core, pl.ds(at, TOK), :] * keep_scale).astype(BF)
        give_out[s, 0:64, :] = (kvg[1 - core, oth_half, :] * give_scale).astype(BF)
        give_out[s, 64:128, :] = (kvg[1 - core, own_half, :] * give_scale).astype(BF)
        dq_out[s, 0:64, :] = dqs[of, 0:128].astype(BF)
        dq_out[s, 64:128, :] = pltpu.roll(dqs[of, 128:256], DR, 1).astype(BF)
        turned = pltpu.roll(dr[own_half, :], DR, 1)
        rope_out[s, :, :] = (jnp.where(low, turned, dr[oth_half, :]) * scale).astype(BF)


def attend(orders, own, other, w_uk, w_uv):
    whole = pl.BlockSpec(memory_space=pltpu.VMEM)
    anywhere = pl.BlockSpec(memory_space=pl.ANY)
    return pl.pallas_call(
        attend_kernel,
        in_specs=[pl.BlockSpec(memory_space=pltpu.SMEM), whole, whole, anywhere, anywhere],
        out_specs=[whole, whole, whole, whole],
        out_shape=[
            jax.ShapeDtypeStruct((16, TOK, 128), BF),
            jax.ShapeDtypeStruct((16, TOK, 128), BF),
            jax.ShapeDtypeStruct((16, TOK, 128), BF),
            jax.ShapeDtypeStruct((16, HALF, 128), BF),
        ],
        scratch_shapes=[
            pltpu.VMEM((DL, 256), BF),
            pltpu.VMEM((2, 2048, 128), BF),
            pltpu.VMEM((2048, 128), BF),
            pltpu.VMEM((256, 2048), BF),
            pltpu.VMEM((1024, 256), BF),
            pltpu.VMEM((1024, 128), BF),
            pltpu.VMEM((2048, 256), F32),
            pltpu.VMEM((2048, 256), F32),
            pltpu.VMEM((2048, 256), BF),
            pltpu.VMEM((2, 2048, 128), F32),
            pltpu.VMEM((2048, 128), F32),
            pltpu.VMEM((1024, 256), F32),
            pltpu.SMEM((16,), jnp.int32),
            pltpu.SemaphoreType.DMA((2,)),
        ],
        compiler_params=pltpu.CompilerParams(vmem_limit_bytes=20 << 20),
    )(orders, own, other, w_uk, w_uv)


def small(kernel, inputs, outputs):
    whole = pl.BlockSpec(memory_space=pltpu.VMEM)
    return pl.pallas_call(
        kernel,
        in_specs=[whole] * len(inputs),
        out_specs=[whole] * len(outputs),
        out_shape=[jax.ShapeDtypeStruct(shape, dtype) for shape, dtype in outputs],
        compiler_params=pltpu.CompilerParams(vmem_limit_bytes=16 << 20),
    )(*inputs)


def finish_kernel(keep_ref, met_ref, rope_ref, dq_ref, own_ref, oth_ref, out_ref):
    total = jnp.zeros((128, DL), F32)
    for i in range(0, 16, 2):
        pair = keep_ref[i : i + 2].astype(F32) + met_ref[i : i + 2].astype(F32)
        out_ref[i : i + 2, 0:128, :] = pair.astype(BF)
        out_ref[i : i + 2, 128:192, :] = rope_ref[i : i + 2]
        out_ref[i : i + 2, 192:256, :] = dq_ref[i : i + 2, 0:64, :]
        lat = jnp.concatenate(
            [
                jnp.concatenate([ref[j, t * HALF : (t + 1) * HALF, :] for t in range(4)], axis=1)
                for j in (i, i + 1)
                for ref in (own_ref, oth_ref)
            ],
            axis=0,
        )
        total = total + dot(pair.reshape(256, 128).T.astype(BF), lat)
    total = total.T
    turned = pltpu.roll(total, DR, 1)
    low = low_lanes((32, TOK))
    for i in range(16):
        for part, first in ((turned, 64), (total, 96)):
            dq = dq_ref[i, first : first + 32, :].astype(F32)
            out_ref[i, 192 + first : 224 + first, :] = jnp.where(low, dq, part[i * 32 : i * 32 + 32]).astype(BF)


def latent_kernel(r_ref, uk_ref, uv_ref, own_out, first_out, second_out, third_out, all_s):
    keys = jnp.concatenate([r_ref[i, 0:128, :] for i in range(0, 16, 2)], axis=1)
    values = jnp.concatenate(
        [jnp.concatenate([r_ref[i, 64:128, :], r_ref[i, 0:64, :]], axis=0) for i in range(1, 16, 2)], axis=1
    )
    all_s[:DL, :] = (dot_nt(uk_ref[...], keys) + dot_nt(uv_ref[...], values)).astype(BF)
    even = r_ref[0, 128:192, :].astype(F32)
    odd = r_ref[1, 128:192, :].astype(F32)
    for i in range(2, 16, 2):
        even = even + r_ref[i, 128:192, :].astype(F32)
        odd = odd + r_ref[i + 1, 128:192, :].astype(F32)
    rope = even + pltpu.roll(odd, DR, 1)
    rope = jnp.concatenate([rope, pltpu.roll(rope, DR, 1)], axis=0).T
    all_s[DL:, :] = rope[:DR, :].astype(BF)
    mine = lax.axis_index("head") // 4
    for k, out in enumerate((own_out, first_out, second_out, third_out)):
        out[...] = all_s[pl.ds(pl.multiple_of((mine ^ k) * PART, 16), PART), :]


def latent_terms(received, w_uk, w_uv):
    whole = pl.BlockSpec(memory_space=pltpu.VMEM)
    return pl.pallas_call(
        latent_kernel,
        in_specs=[whole] * 3,
        out_specs=[whole] * 4,
        out_shape=[jax.ShapeDtypeStruct((PART, TOK), BF)] * 4,
        scratch_shapes=[pltpu.VMEM((DL + DR, TOK), BF)],
        compiler_params=pltpu.CompilerParams(vmem_limit_bytes=16 << 20),
    )(received, w_uk, w_uv)


def four_kernel(a_ref, b_ref, c_ref, d_ref, out_ref):
    first = a_ref[...].astype(F32) + b_ref[...].astype(F32)
    out_ref[...] = (first + (c_ref[...].astype(F32) + d_ref[...].astype(F32))).astype(BF)


def place_kernel(a_ref, b_ref, c_ref, d_ref, out_ref):
    mine = lax.axis_index("head") // 4
    for k, ref in enumerate((a_ref, b_ref, c_ref, d_ref)):
        out_ref[pl.ds(pl.multiple_of((mine ^ k) * PART, 16), PART), :] = ref[...].astype(F32)


def unpack_kernel(r_ref, q_ref, uk_ref, uv_ref):
    low = low_lanes((HALF, TOK))
    for h in range(0, 8, 2):
        for c in range(2):
            rows = slice(c * HALF, c * HALF + HALF)
            i, j, at = 2 * h + c, 2 * h + 2 + c, h * 192
            q_ref[rows, at : at + 128] = r_ref[i, 192:256, :]
            first = r_ref[i, 256:320, :].astype(F32)
            second = pltpu.roll(r_ref[j, 256:320, :].astype(F32), DR, 1)
            turned = pltpu.roll(r_ref[j, 192:256, :].astype(F32), DR, 1)
            q_ref[rows, at + 128 : at + 256] = jnp.where(low, first, turned).astype(BF)
            q_ref[rows, at + 256 : at + 384] = jnp.where(low, turned, second).astype(BF)
    for i in range(16):
        left = pltpu.roll(r_ref[i, 256:288, :].astype(F32), DR, 1)
        right = r_ref[i, 288:320, :].astype(F32)
        ref = uv_ref if i % 2 else uk_ref
        ref[:, (i // 2) * 128 : (i // 2) * 128 + 128] = jnp.where(low[0:32], left, right)


def local(queries, latent, w_uk, w_uv, grad_out, positions, tool_result):
    every = [list(range(16))]
    swap = [(i, i ^ 1) for i in range(16)]

    def exchange(x):
        return lax.all_to_all(x, "ctx", 0, 0, tiled=True, axis_index_groups=every)

    def along_x(x, k):
        return lax.ppermute(x, "head", [(i, i ^ (4 * k)) for i in range(16)])

    def along_z(x, k):
        return lax.ppermute(x, "head", [(i, i ^ k) for i in range(16)])

    own = exchange(pack(queries, latent.T, grad_out, positions, tool_result))
    other = lax.ppermute(own, "ctx", swap)
    orders = own[:, 448, 0].astype(jnp.int32)
    keep, give, dq, rope = attend(orders, own, other, w_uk, w_uv)
    met = lax.ppermute(give, "ctx", swap)
    (back,) = small(finish_kernel, (keep, met, rope, dq, own, other), [((16, BACK, 128), BF)])
    received = exchange(back)
    parts = latent_terms(received, w_uk, w_uv)
    (part,) = small(four_kernel, [parts[0]] + [along_x(parts[k], k) for k in (1, 2, 3)], [((PART, TOK), BF)])
    (part,) = small(four_kernel, [part] + [along_z(part, k) for k in (1, 2, 3)], [((PART, TOK), BF)])
    (whole,) = small(place_kernel, [part] + [along_x(part, k) for k in (1, 2, 3)], [((DL + DR, TOK), F32)])

    grad_queries, grad_w_uk, grad_w_uv = small(
        unpack_kernel, (received,), [((TOK, 1536), BF), ((32, 1024), F32), ((32, 1024), F32)]
    )
    return (grad_queries, whole.T, grad_w_uk, grad_w_uv)


def solution(mesh):
    placed = (
        P("ctx", "head"),
        P("ctx", None),
        P(None, "head"),
        P(None, "head"),
        P("ctx", "head"),
        P("ctx"),
        P("ctx"),
    )
    return jax.shard_map(
        local,
        mesh=mesh,
        in_specs=placed,
        out_specs=(P("ctx", "head"), P("ctx", None), P("ctx", "head"), P("ctx", "head")),
        check_vma=False,
    )
```

```python
import functools
import math

import jax
import jax.numpy as jnp
from jax import lax
from jax.experimental import pallas as pl
from jax.experimental.pallas import tpu as pltpu
from jax.sharding import PartitionSpec as P

DL = 512
DR = 64
DN = 128
DV = 128
TOK = 128
HALF = TOK // 2
ROWS = 464
BACK = 288
PART = (DL + DR) // 4
CHUNK = 512
MASKED = -1e30
BF = jnp.bfloat16
F32 = jnp.float32


def dot(a, b):
    return lax.dot_general(a, b, (((1,), (0,)), ((), ())), preferred_element_type=F32)


def dot_nt(a, b):
    return lax.dot_general(a, b, (((1,), (1,)), ((), ())), preferred_element_type=F32)


def low_lanes(shape):
    return lax.broadcasted_iota(jnp.int32, shape, len(shape) - 1) < DR


def pack_kernel(q_hbm, lat_hbm, g_hbm, pos_hbm, tool_hbm, out_ref, q_ref, lat_ref, g_ref, pos_ref, tool_ref, sems):
    pairs = [(tool_hbm, tool_ref), (pos_hbm, pos_ref), (lat_hbm, lat_ref), (q_hbm, q_ref), (g_hbm, g_ref)]
    copies = [pltpu.make_async_copy(src, dst, sems.at[i]) for i, (src, dst) in enumerate(pairs)]
    for copy in copies:
        copy.start()
    for copy in copies[:3]:
        copy.wait()
    tokens = lat_ref[:DL, :].astype(F32).T.astype(BF)
    rope = jnp.concatenate([jnp.zeros((DR, TOK), F32), lat_ref[DL:, :].astype(F32)], axis=0).T
    keep = jnp.broadcast_to((1 - tool_ref[...]).astype(F32), (TOK, TOK)).T
    order = jnp.broadcast_to((pos_ref[...] // TOK).astype(F32), (16, TOK)).astype(BF)
    halves = [slice(c * HALF, c * HALF + HALF) for c in range(2)]
    for i in range(16):
        for t in range(4):
            out_ref[i, t * HALF : (t + 1) * HALF, :] = tokens[halves[i % 2], t * 128 : (t + 1) * 128]
        out_ref[i, 448:464, :] = order
    for copy in copies[3:]:
        copy.wait()
    low = low_lanes((TOK, TOK))
    for h in range(0, 8, 2):
        at = h * 192
        near = q_ref[:, at + 128 : at + 256].astype(F32)
        mid = pltpu.roll(near, DR, 1)
        end = pltpu.roll(q_ref[:, at + 256 : at + 384].astype(F32), DR, 1)
        nope = [q_ref[:, at : at + 128], jnp.where(low, mid, end).astype(BF)]
        ropes = [jnp.where(low, near, rope).astype(BF), jnp.where(low, end, rope).astype(BF)]
        for k in range(2):
            cotangent = (g_ref[:, (h + k) * 128 : (h + k) * 128 + 128].astype(F32) * keep).astype(BF)
            for c, rows in enumerate(halves):
                to = 2 * (h + k) + c
                out_ref[to, 256:320, :] = ropes[k][rows]
                out_ref[to, 320:384, :] = nope[k][rows]
                out_ref[to, 384:448, :] = cotangent[rows]


def pack(queries, lat_t, grad_out, positions, tool_result):
    return pl.pallas_call(
        pack_kernel,
        in_specs=[pl.BlockSpec(memory_space=pl.ANY)] * 5,
        out_specs=pl.BlockSpec(memory_space=pltpu.VMEM),
        out_shape=jax.ShapeDtypeStruct((16, ROWS, 128), BF),
        scratch_shapes=[
            pltpu.VMEM((TOK, 1536), BF),
            pltpu.VMEM((DL + DR, TOK), BF),
            pltpu.VMEM((TOK, 1024), BF),
            pltpu.VMEM((1, TOK), jnp.int32),
            pltpu.VMEM((1, TOK), jnp.int32),
            pltpu.SemaphoreType.DMA((5,)),
        ],
        compiler_params=pltpu.CompilerParams(vmem_limit_bytes=60 << 20),
    )(queries, lat_t, grad_out, positions.reshape(1, TOK), tool_result.reshape(1, TOK))


def attend_kernel(ord_ref, own_ref, oth_ref, uk_ref, uv_ref, keep_out, give_out, dq_out, rope_out,
                  weights, kv, ts, kt, qs, cs, s_sc, g_sc, ds_sc, p_sc, kvg, dr, dqs, source, sems):
    scale = (DN + DR) ** -0.5
    me = lax.axis_index("ctx")
    core = lax.rem(me, 2)
    columns = pl.ds(pl.multiple_of((me // 2) * 128, 128), 128)
    copies = [
        pltpu.make_async_copy(ref.at[:, columns], weights.at[:, i * 128 : i * 128 + 128], sems.at[i])
        for i, ref in enumerate((uk_ref, uv_ref))
    ]
    for copy in copies:
        copy.start()
    for s in range(16):
        source[ord_ref[s]] = s

    low = low_lanes((HALF, TOK))
    for b in range(16):
        rows = slice(b * HALF, (b + 1) * HALF)
        turned = pltpu.roll(own_ref[source[b], 256:320, :].astype(F32), DR, 1)
        qs[rows, 0:128] = own_ref[source[b], 320:384, :]
        qs[rows, 128:256] = jnp.where(low, 0.0, turned).astype(BF)
        cs[rows, :] = own_ref[source[b], 384:448, :]
    for copy in copies:
        copy.wait()
    for b in range(8):
        rows = slice(b * 256, b * 256 + 256)
        four = [(ref, source[2 * b + k]) for k in range(2) for ref in (own_ref, oth_ref)]
        tokens = jnp.concatenate(
            [
                jnp.concatenate([ref[i, t * HALF : (t + 1) * HALF, :] for t in range(4)], axis=1)
                for ref, i in four
            ],
            axis=0,
        )
        both = dot(tokens, weights[...])
        rope = jnp.concatenate([ref[i, 256:320, :] for ref, i in four], axis=0)
        keys = both[:, 0:128].astype(BF)
        kv[0, rows, :] = keys
        kv[1, rows, :] = both[:, 128:256].astype(BF)
        ts[rows, :] = rope
        kt[0:128, rows] = keys.astype(F32).T.astype(BF)
        kt[128:256, rows] = rope.astype(F32).T.astype(BF)

    factor = scale * math.log2(math.e)
    lane = lax.broadcasted_iota(jnp.int32, (CHUNK, 256), 1)
    qpos = (lane // HALF) * TOK + core * HALF + lax.rem(lane, HALF)
    row = lax.broadcasted_iota(jnp.int32, (CHUNK, 256), 0)
    kpos = (row // TOK) * TOK + lax.rem(lax.rem(row, TOK) + core * HALF, TOK)
    visible = kpos <= qpos
    spans = [slice(c * CHUNK, (c + 1) * CHUNK) for c in range(4)]

    def score(p, c):
        rows, at = slice(p * 256, p * 256 + 256), spans[c]
        s = dot_nt(jnp.concatenate([kv[0, at, :], ts[at, :]], axis=1), qs[rows, :]) * factor
        if c == p:
            s = jnp.where(visible, s, MASKED)
        s_sc[p % 2, at, :] = s
        g_sc[p % 2, at, :] = dot_nt(kv[1, at, :], cs[rows, :])
        return jnp.max(s.reshape(CHUNK // 8, 8, 256), axis=0)

    tops = [score(0, 0)]
    for p in range(4):
        rows = slice(p * 256, p * 256 + 256)
        top = functools.reduce(jnp.maximum, tops)
        tops = []
        top = jnp.max(top, axis=0, keepdims=True)
        total = jnp.zeros((8, 256), F32)
        mixed = jnp.zeros((8, 256), F32)
        for c in range(p + 1):
            at = spans[c]
            e = jnp.exp2(s_sc[p % 2, at, :] - top)
            s_sc[p % 2, at, :] = e
            total = total + jnp.sum(e.reshape(CHUNK // 8, 8, 256), axis=0)
            mixed = mixed + jnp.sum((e * g_sc[p % 2, at, :]).reshape(CHUNK // 8, 8, 256), axis=0)
            if p < 3:
                tops.append(score(p + 1, c))
        share = 1.0 / jnp.sum(total, axis=0, keepdims=True)
        delta = jnp.sum(mixed, axis=0, keepdims=True) * share
        if p < 3:
            tops.append(score(p + 1, p + 1))
        for c in range(p + 1):
            at = spans[c]
            prob = s_sc[p % 2, at, :] * share
            ds_sc[at, rows] = (prob * (g_sc[p % 2, at, :] - delta)).astype(BF)
            p_sc[at, rows] = prob.astype(BF)
        upto = (p + 1) * CHUNK
        dqs[rows, :] = (dot(kt[:, 0:upto], ds_sc[0:upto, rows]) * scale).T
    for c in range(4):
        at = spans[c]
        key_part = dot(ds_sc[at, c * 256 :], qs[c * 256 :, :])
        kvg[0, at, :] = key_part[:, 0:128]
        dr[at, :] = key_part[:, 128:256]
        kvg[1, at, :] = dot(p_sc[at, c * 256 :], cs[c * 256 :, :])

    keep_scale = jnp.where(core == 0, scale, 1.0)
    give_scale = jnp.where(core == 0, 1.0, scale)
    for s in range(16):
        at = pl.multiple_of(ord_ref[s] * TOK, TOK)
        own_half, oth_half = pl.ds(at, HALF), pl.ds(at + HALF, HALF)
        of = pl.ds(pl.multiple_of(ord_ref[s] * HALF, HALF), HALF)
        keep_out[s, :, :] = (kvg[core, pl.ds(at, TOK), :] * keep_scale).astype(BF)
        give_out[s, 0:64, :] = (kvg[1 - core, oth_half, :] * give_scale).astype(BF)
        give_out[s, 64:128, :] = (kvg[1 - core, own_half, :] * give_scale).astype(BF)
        give_out[s, 128:192, :] = (dr[oth_half, :] * scale).astype(BF)
        dq_out[s, :, :] = dqs[of, 0:128].astype(BF)
        turned = pltpu.roll(dqs[of, 128:256], DR, 1)
        rope_out[s, :, :] = jnp.where(low, turned, dr[own_half, :] * scale).astype(BF)


def attend(orders, own, other, w_uk, w_uv):
    whole = pl.BlockSpec(memory_space=pltpu.VMEM)
    anywhere = pl.BlockSpec(memory_space=pl.ANY)
    return pl.pallas_call(
        attend_kernel,
        in_specs=[pl.BlockSpec(memory_space=pltpu.SMEM), whole, whole, anywhere, anywhere],
        out_specs=[whole, whole, whole, whole],
        out_shape=[
            jax.ShapeDtypeStruct((16, TOK, 128), BF),
            jax.ShapeDtypeStruct((16, TOK + HALF, 128), BF),
            jax.ShapeDtypeStruct((16, HALF, 128), BF),
            jax.ShapeDtypeStruct((16, HALF, 128), BF),
        ],
        scratch_shapes=[
            pltpu.VMEM((DL, 256), BF),
            pltpu.VMEM((2, 2048, 128), BF),
            pltpu.VMEM((2048, 128), BF),
            pltpu.VMEM((256, 2048), BF),
            pltpu.VMEM((1024, 256), BF),
            pltpu.VMEM((1024, 128), BF),
            pltpu.VMEM((2, 2048, 256), F32),
            pltpu.VMEM((2, 2048, 256), F32),
            pltpu.VMEM((2048, 1024), BF),
            pltpu.VMEM((2048, 1024), BF),
            pltpu.VMEM((2, 2048, 128), F32),
            pltpu.VMEM((2048, 128), F32),
            pltpu.VMEM((1024, 256), F32),
            pltpu.SMEM((16,), jnp.int32),
            pltpu.SemaphoreType.DMA((2,)),
        ],
        compiler_params=pltpu.CompilerParams(vmem_limit_bytes=32 << 20),
    )(orders, own, other, w_uk, w_uv)


def small(kernel, inputs, outputs):
    whole = pl.BlockSpec(memory_space=pltpu.VMEM)
    return pl.pallas_call(
        kernel,
        in_specs=[whole] * len(inputs),
        out_specs=[whole] * len(outputs),
        out_shape=[jax.ShapeDtypeStruct(shape, dtype) for shape, dtype in outputs],
        compiler_params=pltpu.CompilerParams(vmem_limit_bytes=16 << 20),
    )(*inputs)


def finish_kernel(keep_ref, met_ref, rope_ref, dq_ref, own_ref, oth_ref, out_ref):
    total = jnp.zeros((128, DL), F32)
    for i in range(0, 16, 2):
        pair = keep_ref[i : i + 2].astype(F32) + met_ref[i : i + 2, 0:128, :].astype(F32)
        out_ref[i : i + 2, 0:128, :] = pair.astype(BF)
        rope = rope_ref[i : i + 2].astype(F32) + met_ref[i : i + 2, 128:192, :].astype(F32)
        out_ref[i : i + 2, 128:192, :] = dq_ref[i : i + 2]
        out_ref[i : i + 2, 192:256, :] = rope.astype(BF)
        lat = jnp.concatenate(
            [
                jnp.concatenate([ref[j, t * HALF : (t + 1) * HALF, :] for t in range(4)], axis=1)
                for j in (i, i + 1)
                for ref in (own_ref, oth_ref)
            ],
            axis=0,
        )
        total = total + dot(pair.reshape(256, 128).T.astype(BF), lat)
    out_ref[:, 256:288, :] = total.T.reshape(16, 32, 128).astype(BF)


def latent_kernel(r_ref, uk_ref, uv_ref, own_out, first_out, second_out, third_out, all_s):
    keys = jnp.concatenate([r_ref[i, 0:128, :] for i in range(0, 16, 2)], axis=1)
    values = jnp.concatenate(
        [jnp.concatenate([r_ref[i, 64:128, :], r_ref[i, 0:64, :]], axis=0) for i in range(1, 16, 2)], axis=1
    )
    all_s[:DL, :] = (dot_nt(uk_ref[...], keys) + dot_nt(uv_ref[...], values)).astype(BF)
    halves = [r_ref[c, 192:256, :].astype(F32) for c in range(2)]
    for i in range(2, 16):
        halves[i % 2] = halves[i % 2] + r_ref[i, 192:256, :].astype(F32)
    all_s[DL:, :] = jnp.concatenate(halves, axis=0).T[DR:, :].astype(BF)
    mine = lax.axis_index("head") // 4
    for k, out in enumerate((own_out, first_out, second_out, third_out)):
        out[...] = all_s[pl.ds(pl.multiple_of((mine ^ k) * PART, 16), PART), :]


def latent_terms(received, w_uk, w_uv):
    whole = pl.BlockSpec(memory_space=pltpu.VMEM)
    return pl.pallas_call(
        latent_kernel,
        in_specs=[whole] * 3,
        out_specs=[whole] * 4,
        out_shape=[jax.ShapeDtypeStruct((PART, TOK), BF)] * 4,
        scratch_shapes=[pltpu.VMEM((DL + DR, TOK), BF)],
        compiler_params=pltpu.CompilerParams(vmem_limit_bytes=16 << 20),
    )(received, w_uk, w_uv)


def four_kernel(a_ref, b_ref, c_ref, d_ref, out_ref):
    first = a_ref[...].astype(F32) + b_ref[...].astype(F32)
    out_ref[...] = (first + (c_ref[...].astype(F32) + d_ref[...].astype(F32))).astype(BF)


def place_kernel(a_ref, b_ref, c_ref, d_ref, out_ref):
    mine = lax.axis_index("head") // 4
    for k, ref in enumerate((a_ref, b_ref, c_ref, d_ref)):
        out_ref[pl.ds(pl.multiple_of((mine ^ k) * PART, 16), PART), :] = ref[...].astype(F32)


def unpack_kernel(r_ref, q_ref, uk_ref, uv_ref):
    low = low_lanes((HALF, TOK))
    for h in range(0, 8, 2):
        for c in range(2):
            rows = slice(c * HALF, c * HALF + HALF)
            i, j, at = 2 * h + c, 2 * h + 2 + c, h * 192
            q_ref[rows, at : at + 128] = r_ref[i, 128:192, :]
            first = r_ref[i, 192:256, :].astype(F32)
            second = pltpu.roll(r_ref[j, 192:256, :].astype(F32), DR, 1)
            turned = pltpu.roll(r_ref[j, 128:192, :].astype(F32), DR, 1)
            q_ref[rows, at + 128 : at + 256] = jnp.where(low, first, turned).astype(BF)
            q_ref[rows, at + 256 : at + 384] = jnp.where(low, turned, second).astype(BF)
    for i in range(16):
        ref = uv_ref if i % 2 else uk_ref
        ref[:, (i // 2) * 128 : (i // 2) * 128 + 128] = r_ref[i, 256:288, :].astype(F32)


def local(queries, latent, w_uk, w_uv, grad_out, positions, tool_result):
    every = [list(range(16))]
    swap = [(i, i ^ 1) for i in range(16)]

    def exchange(x):
        return lax.all_to_all(x, "ctx", 0, 0, tiled=True, axis_index_groups=every)

    def along_x(x, k):
        return lax.ppermute(x, "head", [(i, i ^ (4 * k)) for i in range(16)])

    def along_z(x, k):
        return lax.ppermute(x, "head", [(i, i ^ k) for i in range(16)])

    own = exchange(pack(queries, latent.T, grad_out, positions, tool_result))
    other = lax.ppermute(own, "ctx", swap)
    orders = own[:, 448, 0].astype(jnp.int32)
    keep, give, dq, rope = attend(orders, own, other, w_uk, w_uv)
    met = lax.ppermute(give, "ctx", swap)
    (back,) = small(finish_kernel, (keep, met, rope, dq, own, other), [((16, BACK, 128), BF)])
    received = exchange(back)
    parts = latent_terms(received, w_uk, w_uv)
    (part,) = small(four_kernel, [parts[0]] + [along_x(parts[k], k) for k in (1, 2, 3)], [((PART, TOK), BF)])
    (part,) = small(four_kernel, [part] + [along_z(part, k) for k in (1, 2, 3)], [((PART, TOK), BF)])
    (whole,) = small(place_kernel, [part] + [along_x(part, k) for k in (1, 2, 3)], [((DL + DR, TOK), F32)])

    grad_queries, grad_w_uk, grad_w_uv = small(
        unpack_kernel, (received,), [((TOK, 1536), BF), ((32, 1024), F32), ((32, 1024), F32)]
    )
    return (grad_queries, whole.T, grad_w_uk, grad_w_uv)


def solution(mesh):
    placed = (
        P("ctx", "head"),
        P("ctx", None),
        P(None, "head"),
        P(None, "head"),
        P("ctx", "head"),
        P("ctx"),
        P("ctx"),
    )
    return jax.shard_map(
        local,
        mesh=mesh,
        in_specs=placed,
        out_specs=(P("ctx", "head"), P("ctx", None), P("ctx", "head"), P("ctx", "head")),
        check_vma=False,
    )
```

```python
import functools
import math

import jax
import jax.numpy as jnp
from jax import lax
from jax.experimental import pallas as pl
from jax.experimental.pallas import tpu as pltpu
from jax.sharding import PartitionSpec as P

DL = 512
DR = 64
DN = 128
DV = 128
TOK = 128
HALF = TOK // 2
ROWS = 464
BACK = 288
PART = (DL + DR) // 4
MASKED = -1e30
BF = jnp.bfloat16
F32 = jnp.float32


def dot(a, b):
    return lax.dot_general(a, b, (((1,), (0,)), ((), ())), preferred_element_type=F32)


def dot_nt(a, b):
    return lax.dot_general(a, b, (((1,), (1,)), ((), ())), preferred_element_type=F32)


def low_lanes(shape):
    return lax.broadcasted_iota(jnp.int32, shape, len(shape) - 1) < DR


def pack_kernel(q_hbm, lat_hbm, g_hbm, pos_hbm, tool_hbm, out_ref, q_ref, lat_ref, g_ref, pos_ref, tool_ref, sems):
    pairs = [(tool_hbm, tool_ref), (pos_hbm, pos_ref), (lat_hbm, lat_ref), (q_hbm, q_ref), (g_hbm, g_ref)]
    copies = [pltpu.make_async_copy(src, dst, sems.at[i]) for i, (src, dst) in enumerate(pairs)]
    for copy in copies:
        copy.start()
    for copy in copies[:3]:
        copy.wait()
    tokens = lat_ref[:DL, :].astype(F32).T.astype(BF)
    rope = jnp.concatenate([jnp.zeros((DR, TOK), F32), lat_ref[DL:, :].astype(F32)], axis=0).T
    keep = jnp.broadcast_to((1 - tool_ref[...]).astype(F32), (TOK, TOK)).T
    order = jnp.broadcast_to((pos_ref[...] // TOK).astype(F32), (16, TOK)).astype(BF)
    halves = [slice(c * HALF, c * HALF + HALF) for c in range(2)]
    for i in range(16):
        for t in range(4):
            out_ref[i, t * HALF : (t + 1) * HALF, :] = tokens[halves[i % 2], t * 128 : (t + 1) * 128]
        out_ref[i, 448:464, :] = order
    for copy in copies[3:]:
        copy.wait()
    low = low_lanes((TOK, TOK))
    for h in range(0, 8, 2):
        at = h * 192
        near = q_ref[:, at + 128 : at + 256].astype(F32)
        mid = pltpu.roll(near, DR, 1)
        end = pltpu.roll(q_ref[:, at + 256 : at + 384].astype(F32), DR, 1)
        nope = [q_ref[:, at : at + 128], jnp.where(low, mid, end).astype(BF)]
        ropes = [jnp.where(low, near, rope).astype(BF), jnp.where(low, end, rope).astype(BF)]
        for k in range(2):
            cotangent = (g_ref[:, (h + k) * 128 : (h + k) * 128 + 128].astype(F32) * keep).astype(BF)
            for c, rows in enumerate(halves):
                to = 2 * (h + k) + c
                out_ref[to, 256:320, :] = ropes[k][rows]
                out_ref[to, 320:384, :] = nope[k][rows]
                out_ref[to, 384:448, :] = cotangent[rows]


def pack(queries, lat_t, grad_out, positions, tool_result):
    return pl.pallas_call(
        pack_kernel,
        in_specs=[pl.BlockSpec(memory_space=pl.ANY)] * 5,
        out_specs=pl.BlockSpec(memory_space=pltpu.VMEM),
        out_shape=jax.ShapeDtypeStruct((16, ROWS, 128), BF),
        scratch_shapes=[
            pltpu.VMEM((TOK, 1536), BF),
            pltpu.VMEM((DL + DR, TOK), BF),
            pltpu.VMEM((TOK, 1024), BF),
            pltpu.VMEM((1, TOK), jnp.int32),
            pltpu.VMEM((1, TOK), jnp.int32),
            pltpu.SemaphoreType.DMA((5,)),
        ],
        compiler_params=pltpu.CompilerParams(vmem_limit_bytes=60 << 20),
    )(queries, lat_t, grad_out, positions.reshape(1, TOK), tool_result.reshape(1, TOK))


FACTOR = (DN + DR) ** -0.5 * math.log2(math.e)


def project(ref, source, weights, keys, values, ropes, turned):
    for b in range(4):
        rows = slice(b * 256, b * 256 + 256)
        four = [source[4 * b + k] for k in range(4)]
        tokens = jnp.concatenate(
            [jnp.concatenate([ref[i, t * HALF : (t + 1) * HALF, :] for t in range(4)], axis=1) for i in four], axis=0
        )
        both = dot(tokens, weights[...])
        rope = jnp.concatenate([ref[i, 256:320, :] for i in four], axis=0)
        key = both[:, 0:128].astype(BF)
        keys[rows, :] = key
        values[rows, :] = both[:, 128:256].astype(BF)
        ropes[rows, :] = rope
        turned[0:128, rows] = key.astype(F32).T.astype(BF)
        turned[128:256, rows] = rope.astype(F32).T.astype(BF)


def fetch_weights(uk_ref, uv_ref, weights, sems):
    columns = pl.ds(pl.multiple_of((lax.axis_index("ctx") // 2) * 128, 128), 128)
    copies = [
        pltpu.make_async_copy(ref.at[:, columns], weights.at[:, i * 128 : i * 128 + 128], sems.at[i])
        for i, ref in enumerate((uk_ref, uv_ref))
    ]
    for copy in copies:
        copy.start()
    return copies


def own_kernel(ord_ref, own_ref, uk_ref, uv_ref, qs, cs, keys, values, ropes, turned, s_out, g_out, top_out,
               weights, source, sems):
    copies = fetch_weights(uk_ref, uv_ref, weights, sems)
    for s in range(16):
        source[ord_ref[s]] = s
    low = low_lanes((HALF, TOK))
    for b in range(16):
        rows = slice(b * HALF, (b + 1) * HALF)
        rope = pltpu.roll(own_ref[source[b], 256:320, :].astype(F32), DR, 1)
        qs[rows, 0:128] = own_ref[source[b], 320:384, :]
        qs[rows, 128:256] = jnp.where(low, 0.0, rope).astype(BF)
        cs[rows, :] = own_ref[source[b], 384:448, :]
    for copy in copies:
        copy.wait()
    project(own_ref, source, weights, keys, values, ropes, turned)
    visible = lax.broadcasted_iota(jnp.int32, (256, 256), 0) <= lax.broadcasted_iota(jnp.int32, (256, 256), 1)
    for p in range(4):
        rows, first = slice(p * 256, p * 256 + 256), 128 * p * (p + 1)
        top = jnp.full((8, 256), MASKED, F32)
        for c in range(p + 1):
            at, to = slice(c * 256, c * 256 + 256), slice(first + c * 256, first + c * 256 + 256)
            sc = dot_nt(jnp.concatenate([keys[at, :], ropes[at, :]], axis=1), qs[rows, :]) * FACTOR
            if c == p:
                sc = jnp.where(visible, sc, MASKED)
            s_out[to, :] = sc
            g_out[to, :] = dot_nt(values[at, :], cs[rows, :])
            top = jnp.maximum(top, jnp.max(sc.reshape(32, 8, 256), axis=0))
        top_out[p, :, :] = top


def own_side(orders, own, w_uk, w_uv):
    whole = pl.BlockSpec(memory_space=pltpu.VMEM)
    anywhere = pl.BlockSpec(memory_space=pl.ANY)
    shapes = [(1024, 256), (1024, 128), (1024, 128), (1024, 128), (1024, 128), (256, 1024)]
    return pl.pallas_call(
        own_kernel,
        in_specs=[pl.BlockSpec(memory_space=pltpu.SMEM), whole, anywhere, anywhere],
        out_specs=[whole] * 9,
        out_shape=[jax.ShapeDtypeStruct(shape, BF) for shape in shapes]
        + [jax.ShapeDtypeStruct(shape, F32) for shape in ((2560, 256), (2560, 256), (4, 8, 256))],
        scratch_shapes=[pltpu.VMEM((DL, 256), BF), pltpu.SMEM((16,), jnp.int32), pltpu.SemaphoreType.DMA((2,))],
        compiler_params=pltpu.CompilerParams(vmem_limit_bytes=12 << 20),
    )(orders, own, w_uk, w_uv)


def attend_kernel(ord_ref, oth_ref, uk_ref, uv_ref, qs, cs, own_keys, own_values, own_ropes, own_turned, s_own, g_own,
                  top_own, keep_out, give_out, dq_out, rope_out,
                  weights, keys, values, ropes, turned, s_sc, g_sc, ds_sc, p_sc, kvg, dr, dqs, source, sems):
    scale = (DN + DR) ** -0.5
    core = lax.rem(lax.axis_index("ctx"), 2)
    copies = fetch_weights(uk_ref, uv_ref, weights, sems)
    for s in range(16):
        source[ord_ref[s]] = s
    for copy in copies:
        copy.wait()
    project(oth_ref, source, weights, keys, values, ropes, turned)
    row = lax.broadcasted_iota(jnp.int32, (256, 256), 0) // HALF
    lane = lax.broadcasted_iota(jnp.int32, (256, 256), 1) // HALF
    visible = row < lane + core
    spans = [slice(c * 256, (c + 1) * 256) for c in range(4)]

    def score(p, c):
        at = spans[c]
        sc = dot_nt(jnp.concatenate([keys[at, :], ropes[at, :]], axis=1), qs[spans[p], :]) * FACTOR
        if c == p:
            sc = jnp.where(visible, sc, MASKED)
        s_sc[p % 2, 1, at, :] = sc
        g_sc[p % 2, at, :] = dot_nt(values[at, :], cs[spans[p], :])
        return jnp.max(sc.reshape(32, 8, 256), axis=0)

    tops = [score(0, 0)]
    for p in range(4):
        rows, first = spans[p], 128 * p * (p + 1)
        top = functools.reduce(jnp.maximum, tops, top_own[p])
        tops = []
        top = jnp.max(top, axis=0, keepdims=True)
        total = jnp.zeros((8, 256), F32)
        mixed = jnp.zeros((8, 256), F32)
        for c in range(p + 1):
            at, of = spans[c], slice(first + c * 256, first + c * 256 + 256)
            for side in range(2):
                e = jnp.exp2((s_sc[p % 2, 1, at, :] if side else s_own[of, :]) - top)
                g = g_sc[p % 2, at, :] if side else g_own[of, :]
                s_sc[p % 2, side, at, :] = e
                total = total + jnp.sum(e.reshape(32, 8, 256), axis=0)
                mixed = mixed + jnp.sum((e * g).reshape(32, 8, 256), axis=0)
            if p < 3:
                tops.append(score(p + 1, c))
        share = 1.0 / jnp.sum(total, axis=0, keepdims=True)
        delta = jnp.sum(mixed, axis=0, keepdims=True) * share
        if p < 3:
            tops.append(score(p + 1, p + 1))
        for c in range(p + 1):
            at, of = spans[c], slice(first + c * 256, first + c * 256 + 256)
            for side in range(2):
                prob = s_sc[p % 2, side, at, :] * share
                g = g_sc[p % 2, at, :] if side else g_own[of, :]
                ds_sc[side, at, rows] = (prob * (g - delta)).astype(BF)
                p_sc[side, at, rows] = prob.astype(BF)
        upto = (p + 1) * 256
        dq = dot(own_turned[:, 0:upto], ds_sc[0, 0:upto, rows]) + dot(turned[:, 0:upto], ds_sc[1, 0:upto, rows])
        dqs[rows, :] = (dq * scale).T
    for c in range(4):
        at = spans[c]
        for side in range(2):
            key_part = dot(ds_sc[side, at, c * 256 :], qs[c * 256 :, :])
            kvg[0, side, at, :] = key_part[:, 0:128]
            dr[side, at, :] = key_part[:, 128:256]
            kvg[1, side, at, :] = dot(p_sc[side, at, c * 256 :], cs[c * 256 :, :])

    low = low_lanes((HALF, TOK))
    keep_scale = jnp.where(core == 0, scale, 1.0)
    give_scale = jnp.where(core == 0, 1.0, scale)
    for s in range(16):
        at = pl.ds(pl.multiple_of(ord_ref[s] * HALF, HALF), HALF)
        for side in range(2):
            half = slice(side * HALF, side * HALF + HALF)
            keep_out[s, half, :] = (kvg[core, side, at, :] * keep_scale).astype(BF)
            give_out[s, half, :] = (kvg[1 - core, 1 - side, at, :] * give_scale).astype(BF)
        give_out[s, 128:192, :] = (dr[1, at, :] * scale).astype(BF)
        dq_out[s, :, :] = dqs[at, 0:128].astype(BF)
        moved = pltpu.roll(dqs[at, 128:256], DR, 1)
        rope_out[s, :, :] = jnp.where(low, moved, dr[0, at, :] * scale).astype(BF)


def attend(orders, other, w_uk, w_uv, mine):
    whole = pl.BlockSpec(memory_space=pltpu.VMEM)
    anywhere = pl.BlockSpec(memory_space=pl.ANY)
    return pl.pallas_call(
        attend_kernel,
        in_specs=[pl.BlockSpec(memory_space=pltpu.SMEM), whole, anywhere, anywhere] + [whole] * 9,
        out_specs=[whole, whole, whole, whole],
        out_shape=[
            jax.ShapeDtypeStruct((16, TOK, 128), BF),
            jax.ShapeDtypeStruct((16, TOK + HALF, 128), BF),
            jax.ShapeDtypeStruct((16, HALF, 128), BF),
            jax.ShapeDtypeStruct((16, HALF, 128), BF),
        ],
        scratch_shapes=[
            pltpu.VMEM((DL, 256), BF),
            pltpu.VMEM((1024, 128), BF),
            pltpu.VMEM((1024, 128), BF),
            pltpu.VMEM((1024, 128), BF),
            pltpu.VMEM((256, 1024), BF),
            pltpu.VMEM((2, 2, 1024, 256), F32),
            pltpu.VMEM((2, 1024, 256), F32),
            pltpu.VMEM((2, 1024, 1024), BF),
            pltpu.VMEM((2, 1024, 1024), BF),
            pltpu.VMEM((2, 2, 1024, 128), F32),
            pltpu.VMEM((2, 1024, 128), F32),
            pltpu.VMEM((1024, 256), F32),
            pltpu.SMEM((16,), jnp.int32),
            pltpu.SemaphoreType.DMA((2,)),
        ],
        compiler_params=pltpu.CompilerParams(vmem_limit_bytes=28 << 20),
    )(orders, other, w_uk, w_uv, *mine)


def small(kernel, inputs, outputs):
    whole = pl.BlockSpec(memory_space=pltpu.VMEM)
    return pl.pallas_call(
        kernel,
        in_specs=[whole] * len(inputs),
        out_specs=[whole] * len(outputs),
        out_shape=[jax.ShapeDtypeStruct(shape, dtype) for shape, dtype in outputs],
        compiler_params=pltpu.CompilerParams(vmem_limit_bytes=16 << 20),
    )(*inputs)


def finish_kernel(keep_ref, met_ref, rope_ref, dq_ref, own_ref, oth_ref, out_ref):
    total = jnp.zeros((128, DL), F32)
    for i in range(0, 16, 2):
        pair = keep_ref[i : i + 2].astype(F32) + met_ref[i : i + 2, 0:128, :].astype(F32)
        out_ref[i : i + 2, 0:128, :] = pair.astype(BF)
        rope = rope_ref[i : i + 2].astype(F32) + met_ref[i : i + 2, 128:192, :].astype(F32)
        out_ref[i : i + 2, 128:192, :] = dq_ref[i : i + 2]
        out_ref[i : i + 2, 192:256, :] = rope.astype(BF)
        lat = jnp.concatenate(
            [
                jnp.concatenate([ref[j, t * HALF : (t + 1) * HALF, :] for t in range(4)], axis=1)
                for j in (i, i + 1)
                for ref in (own_ref, oth_ref)
            ],
            axis=0,
        )
        total = total + dot(pair.reshape(256, 128).T.astype(BF), lat)
    out_ref[:, 256:288, :] = total.T.reshape(16, 32, 128).astype(BF)


def latent_kernel(r_ref, uk_ref, uv_ref, own_out, first_out, second_out, third_out, all_s):
    keys = jnp.concatenate([r_ref[i, 0:128, :] for i in range(0, 16, 2)], axis=1)
    values = jnp.concatenate(
        [jnp.concatenate([r_ref[i, 64:128, :], r_ref[i, 0:64, :]], axis=0) for i in range(1, 16, 2)], axis=1
    )
    all_s[:DL, :] = (dot_nt(uk_ref[...], keys) + dot_nt(uv_ref[...], values)).astype(BF)
    halves = [r_ref[c, 192:256, :].astype(F32) for c in range(2)]
    for i in range(2, 16):
        halves[i % 2] = halves[i % 2] + r_ref[i, 192:256, :].astype(F32)
    all_s[DL:, :] = jnp.concatenate(halves, axis=0).T[DR:, :].astype(BF)
    mine = lax.axis_index("head") // 4
    for k, out in enumerate((own_out, first_out, second_out, third_out)):
        out[...] = all_s[pl.ds(pl.multiple_of((mine ^ k) * PART, 16), PART), :]


def latent_terms(received, w_uk, w_uv):
    whole = pl.BlockSpec(memory_space=pltpu.VMEM)
    return pl.pallas_call(
        latent_kernel,
        in_specs=[whole] * 3,
        out_specs=[whole] * 4,
        out_shape=[jax.ShapeDtypeStruct((PART, TOK), BF)] * 4,
        scratch_shapes=[pltpu.VMEM((DL + DR, TOK), BF)],
        compiler_params=pltpu.CompilerParams(vmem_limit_bytes=16 << 20),
    )(received, w_uk, w_uv)


def four_kernel(a_ref, b_ref, c_ref, d_ref, out_ref):
    first = a_ref[...].astype(F32) + b_ref[...].astype(F32)
    out_ref[...] = (first + (c_ref[...].astype(F32) + d_ref[...].astype(F32))).astype(BF)


def place_kernel(a_ref, b_ref, c_ref, d_ref, out_ref):
    mine = lax.axis_index("head") // 4
    for k, ref in enumerate((a_ref, b_ref, c_ref, d_ref)):
        out_ref[pl.ds(pl.multiple_of((mine ^ k) * PART, 16), PART), :] = ref[...].astype(F32)


def unpack_kernel(r_ref, q_ref, uk_ref, uv_ref):
    low = low_lanes((HALF, TOK))
    for h in range(0, 8, 2):
        for c in range(2):
            rows = slice(c * HALF, c * HALF + HALF)
            i, j, at = 2 * h + c, 2 * h + 2 + c, h * 192
            q_ref[rows, at : at + 128] = r_ref[i, 128:192, :]
            first = r_ref[i, 192:256, :].astype(F32)
            second = pltpu.roll(r_ref[j, 192:256, :].astype(F32), DR, 1)
            turned = pltpu.roll(r_ref[j, 128:192, :].astype(F32), DR, 1)
            q_ref[rows, at + 128 : at + 256] = jnp.where(low, first, turned).astype(BF)
            q_ref[rows, at + 256 : at + 384] = jnp.where(low, turned, second).astype(BF)
    for i in range(16):
        ref = uv_ref if i % 2 else uk_ref
        ref[:, (i // 2) * 128 : (i // 2) * 128 + 128] = r_ref[i, 256:288, :].astype(F32)


def local(queries, latent, w_uk, w_uv, grad_out, positions, tool_result):
    every = [list(range(16))]
    swap = [(i, i ^ 1) for i in range(16)]

    def exchange(x):
        return lax.all_to_all(x, "ctx", 0, 0, tiled=True, axis_index_groups=every)

    def along_x(x, k):
        return lax.ppermute(x, "head", [(i, i ^ (4 * k)) for i in range(16)])

    def along_z(x, k):
        return lax.ppermute(x, "head", [(i, i ^ k) for i in range(16)])

    own = exchange(pack(queries, latent.T, grad_out, positions, tool_result))
    other = lax.ppermute(own, "ctx", swap)
    orders = own[:, 448, 0].astype(jnp.int32)
    mine = own_side(orders, own, w_uk, w_uv)
    keep, give, dq, rope = attend(orders, other, w_uk, w_uv, mine)
    met = lax.ppermute(give, "ctx", swap)
    (back,) = small(finish_kernel, (keep, met, rope, dq, own, other), [((16, BACK, 128), BF)])
    received = exchange(back)
    parts = latent_terms(received, w_uk, w_uv)
    (part,) = small(four_kernel, [parts[0]] + [along_x(parts[k], k) for k in (1, 2, 3)], [((PART, TOK), BF)])
    (part,) = small(four_kernel, [part] + [along_z(part, k) for k in (1, 2, 3)], [((PART, TOK), BF)])
    (whole,) = small(place_kernel, [part] + [along_x(part, k) for k in (1, 2, 3)], [((DL + DR, TOK), F32)])

    grad_queries, grad_w_uk, grad_w_uv = small(
        unpack_kernel, (received,), [((TOK, 1536), BF), ((32, 1024), F32), ((32, 1024), F32)]
    )
    return (grad_queries, whole.T, grad_w_uk, grad_w_uv)


def solution(mesh):
    placed = (
        P("ctx", "head"),
        P("ctx", None),
        P(None, "head"),
        P(None, "head"),
        P("ctx", "head"),
        P("ctx"),
        P("ctx"),
    )
    return jax.shard_map(
        local,
        mesh=mesh,
        in_specs=placed,
        out_specs=(P("ctx", "head"), P("ctx", None), P("ctx", "head"), P("ctx", "head")),
        check_vma=False,
    )
```

```python
import functools
import math

import jax
import jax.numpy as jnp
from jax import lax
from jax.experimental import pallas as pl
from jax.experimental.pallas import tpu as pltpu
from jax.sharding import PartitionSpec as P

DL = 512
DR = 64
DN = 128
DV = 128
TOK = 128
HALF = TOK // 2
ROWS = 464
BACK = 288
PART = (DL + DR) // 4
MASKED = -1e30
BF = jnp.bfloat16
F32 = jnp.float32


def dot(a, b):
    return lax.dot_general(a, b, (((1,), (0,)), ((), ())), preferred_element_type=F32)


def dot_nt(a, b):
    return lax.dot_general(a, b, (((1,), (1,)), ((), ())), preferred_element_type=F32)


def low_lanes(shape):
    return lax.broadcasted_iota(jnp.int32, shape, len(shape) - 1) < DR


def pack_kernel(q_hbm, lat_hbm, g_hbm, pos_hbm, tool_hbm, out_ref, q_ref, lat_ref, g_ref, pos_ref, tool_ref, sems):
    pairs = [(tool_hbm, tool_ref), (pos_hbm, pos_ref), (lat_hbm, lat_ref), (q_hbm, q_ref), (g_hbm, g_ref)]
    copies = [pltpu.make_async_copy(src, dst, sems.at[i]) for i, (src, dst) in enumerate(pairs)]
    for copy in copies:
        copy.start()
    for copy in copies[:3]:
        copy.wait()
    tokens = lat_ref[:DL, :].astype(F32).T.astype(BF)
    rope = jnp.concatenate([jnp.zeros((DR, TOK), F32), lat_ref[DL:, :].astype(F32)], axis=0).T
    keep = jnp.broadcast_to((1 - tool_ref[...]).astype(F32), (TOK, TOK)).T
    order = jnp.broadcast_to((pos_ref[...] // TOK).astype(F32), (16, TOK)).astype(BF)
    halves = [slice(c * HALF, c * HALF + HALF) for c in range(2)]
    for i in range(16):
        for t in range(4):
            out_ref[i, t * HALF : (t + 1) * HALF, :] = tokens[halves[i % 2], t * 128 : (t + 1) * 128]
        out_ref[i, 448:464, :] = order
    for copy in copies[3:]:
        copy.wait()
    low = low_lanes((TOK, TOK))
    for h in range(0, 8, 2):
        at = h * 192
        near = q_ref[:, at + 128 : at + 256].astype(F32)
        mid = pltpu.roll(near, DR, 1)
        end = pltpu.roll(q_ref[:, at + 256 : at + 384].astype(F32), DR, 1)
        nope = [q_ref[:, at : at + 128], jnp.where(low, mid, end).astype(BF)]
        ropes = [jnp.where(low, near, rope).astype(BF), jnp.where(low, end, rope).astype(BF)]
        for k in range(2):
            cotangent = (g_ref[:, (h + k) * 128 : (h + k) * 128 + 128].astype(F32) * keep).astype(BF)
            for c, rows in enumerate(halves):
                to = 2 * (h + k) + c
                out_ref[to, 256:320, :] = ropes[k][rows]
                out_ref[to, 320:384, :] = nope[k][rows]
                out_ref[to, 384:448, :] = cotangent[rows]


def pack(queries, lat_t, grad_out, positions, tool_result):
    return pl.pallas_call(
        pack_kernel,
        in_specs=[pl.BlockSpec(memory_space=pl.ANY)] * 5,
        out_specs=pl.BlockSpec(memory_space=pltpu.VMEM),
        out_shape=jax.ShapeDtypeStruct((16, ROWS, 128), BF),
        scratch_shapes=[
            pltpu.VMEM((TOK, 1536), BF),
            pltpu.VMEM((DL + DR, TOK), BF),
            pltpu.VMEM((TOK, 1024), BF),
            pltpu.VMEM((1, TOK), jnp.int32),
            pltpu.VMEM((1, TOK), jnp.int32),
            pltpu.SemaphoreType.DMA((5,)),
        ],
        compiler_params=pltpu.CompilerParams(vmem_limit_bytes=60 << 20),
    )(queries, lat_t, grad_out, positions.reshape(1, TOK), tool_result.reshape(1, TOK))


FACTOR = (DN + DR) ** -0.5 * math.log2(math.e)


def project(ref, source, weights, keys, values, ropes, turned):
    for b in range(4):
        rows = slice(b * 256, b * 256 + 256)
        four = [source[4 * b + k] for k in range(4)]
        tokens = jnp.concatenate(
            [jnp.concatenate([ref[i, t * HALF : (t + 1) * HALF, :] for t in range(4)], axis=1) for i in four], axis=0
        )
        both = dot(tokens, weights[...])
        rope = jnp.concatenate([ref[i, 256:320, :] for i in four], axis=0)
        key = both[:, 0:128].astype(BF)
        keys[rows, :] = key
        values[rows, :] = both[:, 128:256].astype(BF)
        ropes[rows, :] = rope
        turned[0:128, rows] = key.astype(F32).T.astype(BF)
        turned[128:256, rows] = rope.astype(F32).T.astype(BF)


def fetch_weights(uk_ref, uv_ref, weights, sems):
    columns = pl.ds(pl.multiple_of((lax.axis_index("ctx") // 2) * 128, 128), 128)
    copies = [
        pltpu.make_async_copy(ref.at[:, columns], weights.at[:, i * 128 : i * 128 + 128], sems.at[i])
        for i, ref in enumerate((uk_ref, uv_ref))
    ]
    for copy in copies:
        copy.start()
    return copies


def own_kernel(ord_ref, own_ref, uk_ref, uv_ref, qs, cs, keys, values, ropes, turned, s_out, g_out, top_out, total_out,
               mixed_out, weights, source, sems):
    copies = fetch_weights(uk_ref, uv_ref, weights, sems)
    for s in range(16):
        source[ord_ref[s]] = s
    low = low_lanes((HALF, TOK))
    for b in range(16):
        rows = slice(b * HALF, (b + 1) * HALF)
        rope = pltpu.roll(own_ref[source[b], 256:320, :].astype(F32), DR, 1)
        qs[rows, 0:128] = own_ref[source[b], 320:384, :]
        qs[rows, 128:256] = jnp.where(low, 0.0, rope).astype(BF)
        cs[rows, :] = own_ref[source[b], 384:448, :]
    for copy in copies:
        copy.wait()
    project(own_ref, source, weights, keys, values, ropes, turned)
    visible = lax.broadcasted_iota(jnp.int32, (256, 256), 0) <= lax.broadcasted_iota(jnp.int32, (256, 256), 1)
    for p in range(4):
        rows, first = slice(p * 256, p * 256 + 256), 128 * p * (p + 1)
        top = jnp.full((8, 256), MASKED, F32)
        for c in range(p + 1):
            at, to = slice(c * 256, c * 256 + 256), slice(first + c * 256, first + c * 256 + 256)
            sc = dot_nt(jnp.concatenate([keys[at, :], ropes[at, :]], axis=1), qs[rows, :]) * FACTOR
            if c == p:
                sc = jnp.where(visible, sc, MASKED)
            s_out[to, :] = sc
            g_out[to, :] = dot_nt(values[at, :], cs[rows, :])
            top = jnp.maximum(top, jnp.max(sc.reshape(32, 8, 256), axis=0))
        top = jnp.max(top, axis=0, keepdims=True)
        total = jnp.zeros((8, 256), F32)
        mixed = jnp.zeros((8, 256), F32)
        for c in range(p + 1):
            of = slice(first + c * 256, first + c * 256 + 256)
            e = jnp.exp2(s_out[of, :] - top)
            s_out[of, :] = e
            total = total + jnp.sum(e.reshape(32, 8, 256), axis=0)
            mixed = mixed + jnp.sum((e * g_out[of, :]).reshape(32, 8, 256), axis=0)
        top_out[p, :, :] = jnp.broadcast_to(top, (8, 256))
        total_out[p, :, :] = total
        mixed_out[p, :, :] = mixed


def own_side(orders, own, w_uk, w_uv):
    whole = pl.BlockSpec(memory_space=pltpu.VMEM)
    anywhere = pl.BlockSpec(memory_space=pl.ANY)
    shapes = [(1024, 256), (1024, 128), (1024, 128), (1024, 128), (1024, 128), (256, 1024)]
    return pl.pallas_call(
        own_kernel,
        in_specs=[pl.BlockSpec(memory_space=pltpu.SMEM), whole, anywhere, anywhere],
        out_specs=[whole] * 11,
        out_shape=[jax.ShapeDtypeStruct(shape, BF) for shape in shapes]
        + [jax.ShapeDtypeStruct(shape, F32) for shape in ((2560, 256), (2560, 256)) + ((4, 8, 256),) * 3],
        scratch_shapes=[pltpu.VMEM((DL, 256), BF), pltpu.SMEM((16,), jnp.int32), pltpu.SemaphoreType.DMA((2,))],
        compiler_params=pltpu.CompilerParams(vmem_limit_bytes=12 << 20),
    )(orders, own, w_uk, w_uv)


def attend_kernel(ord_ref, oth_ref, uk_ref, uv_ref, qs, cs, own_keys, own_values, own_ropes, own_turned, e_own, g_own,
                  top_own, total_own, mixed_own, keep_out, give_out, dq_out, rope_out,
                  weights, keys, values, ropes, turned, s_sc, g_sc, ds_sc, p_sc, kvg, dr, dqs, source, sems):
    scale = (DN + DR) ** -0.5
    core = lax.rem(lax.axis_index("ctx"), 2)
    copies = fetch_weights(uk_ref, uv_ref, weights, sems)
    for s in range(16):
        source[ord_ref[s]] = s
    for copy in copies:
        copy.wait()
    project(oth_ref, source, weights, keys, values, ropes, turned)
    row = lax.broadcasted_iota(jnp.int32, (256, 256), 0) // HALF
    lane = lax.broadcasted_iota(jnp.int32, (256, 256), 1) // HALF
    visible = row < lane + core
    spans = [slice(c * 256, (c + 1) * 256) for c in range(4)]

    def score(p, c):
        at = spans[c]
        sc = dot_nt(jnp.concatenate([keys[at, :], ropes[at, :]], axis=1), qs[spans[p], :]) * FACTOR
        if c == p:
            sc = jnp.where(visible, sc, MASKED)
        s_sc[p % 2, at, :] = sc
        g_sc[p % 2, at, :] = dot_nt(values[at, :], cs[spans[p], :])
        return jnp.max(sc.reshape(32, 8, 256), axis=0)

    tops = [score(0, 0)]
    for p in range(4):
        rows, first = spans[p], 128 * p * (p + 1)
        top = functools.reduce(jnp.maximum, tops, top_own[p])
        tops = []
        top = jnp.max(top, axis=0, keepdims=True)
        shrink = jnp.exp2(top_own[p] - top)
        total = total_own[p] * shrink
        mixed = mixed_own[p] * shrink
        for c in range(p + 1):
            at = spans[c]
            e = jnp.exp2(s_sc[p % 2, at, :] - top)
            s_sc[p % 2, at, :] = e
            total = total + jnp.sum(e.reshape(32, 8, 256), axis=0)
            mixed = mixed + jnp.sum((e * g_sc[p % 2, at, :]).reshape(32, 8, 256), axis=0)
            if p < 3:
                tops.append(score(p + 1, c))
        share = 1.0 / jnp.sum(total, axis=0, keepdims=True)
        delta = jnp.sum(mixed, axis=0, keepdims=True) * share
        own_share = shrink[0:1] * share
        if p < 3:
            tops.append(score(p + 1, p + 1))
        for c in range(p + 1):
            at, of = spans[c], slice(first + c * 256, first + c * 256 + 256)
            for side in range(2):
                prob = s_sc[p % 2, at, :] * share if side else e_own[of, :] * own_share
                g = g_sc[p % 2, at, :] if side else g_own[of, :]
                ds_sc[side, at, rows] = (prob * (g - delta)).astype(BF)
                p_sc[side, at, rows] = prob.astype(BF)
        upto = (p + 1) * 256
        dq = dot(own_turned[:, 0:upto], ds_sc[0, 0:upto, rows]) + dot(turned[:, 0:upto], ds_sc[1, 0:upto, rows])
        dqs[rows, :] = (dq * scale).T
    for c in range(4):
        at = spans[c]
        for side in range(2):
            key_part = dot(ds_sc[side, at, c * 256 :], qs[c * 256 :, :])
            kvg[0, side, at, :] = key_part[:, 0:128]
            dr[side, at, :] = key_part[:, 128:256]
            kvg[1, side, at, :] = dot(p_sc[side, at, c * 256 :], cs[c * 256 :, :])

    low = low_lanes((HALF, TOK))
    keep_scale = jnp.where(core == 0, scale, 1.0)
    give_scale = jnp.where(core == 0, 1.0, scale)
    for s in range(16):
        at = pl.ds(pl.multiple_of(ord_ref[s] * HALF, HALF), HALF)
        for side in range(2):
            half = slice(side * HALF, side * HALF + HALF)
            keep_out[s, half, :] = (kvg[core, side, at, :] * keep_scale).astype(BF)
            give_out[s, half, :] = (kvg[1 - core, 1 - side, at, :] * give_scale).astype(BF)
        give_out[s, 128:192, :] = (dr[1, at, :] * scale).astype(BF)
        dq_out[s, :, :] = dqs[at, 0:128].astype(BF)
        moved = pltpu.roll(dqs[at, 128:256], DR, 1)
        rope_out[s, :, :] = jnp.where(low, moved, dr[0, at, :] * scale).astype(BF)


def attend(orders, other, w_uk, w_uv, mine):
    whole = pl.BlockSpec(memory_space=pltpu.VMEM)
    anywhere = pl.BlockSpec(memory_space=pl.ANY)
    return pl.pallas_call(
        attend_kernel,
        in_specs=[pl.BlockSpec(memory_space=pltpu.SMEM), whole, anywhere, anywhere] + [whole] * 11,
        out_specs=[whole, whole, whole, whole],
        out_shape=[
            jax.ShapeDtypeStruct((16, TOK, 128), BF),
            jax.ShapeDtypeStruct((16, TOK + HALF, 128), BF),
            jax.ShapeDtypeStruct((16, HALF, 128), BF),
            jax.ShapeDtypeStruct((16, HALF, 128), BF),
        ],
        scratch_shapes=[
            pltpu.VMEM((DL, 256), BF),
            pltpu.VMEM((1024, 128), BF),
            pltpu.VMEM((1024, 128), BF),
            pltpu.VMEM((1024, 128), BF),
            pltpu.VMEM((256, 1024), BF),
            pltpu.VMEM((2, 1024, 256), F32),
            pltpu.VMEM((2, 1024, 256), F32),
            pltpu.VMEM((2, 1024, 1024), BF),
            pltpu.VMEM((2, 1024, 1024), BF),
            pltpu.VMEM((2, 2, 1024, 128), F32),
            pltpu.VMEM((2, 1024, 128), F32),
            pltpu.VMEM((1024, 256), F32),
            pltpu.SMEM((16,), jnp.int32),
            pltpu.SemaphoreType.DMA((2,)),
        ],
        compiler_params=pltpu.CompilerParams(vmem_limit_bytes=28 << 20),
    )(orders, other, w_uk, w_uv, *mine)


def small(kernel, inputs, outputs):
    whole = pl.BlockSpec(memory_space=pltpu.VMEM)
    return pl.pallas_call(
        kernel,
        in_specs=[whole] * len(inputs),
        out_specs=[whole] * len(outputs),
        out_shape=[jax.ShapeDtypeStruct(shape, dtype) for shape, dtype in outputs],
        compiler_params=pltpu.CompilerParams(vmem_limit_bytes=16 << 20),
    )(*inputs)


def finish_kernel(keep_ref, met_ref, rope_ref, dq_ref, own_ref, oth_ref, out_ref):
    total = jnp.zeros((128, DL), F32)
    for i in range(0, 16, 2):
        pair = keep_ref[i : i + 2].astype(F32) + met_ref[i : i + 2, 0:128, :].astype(F32)
        out_ref[i : i + 2, 0:128, :] = pair.astype(BF)
        rope = rope_ref[i : i + 2].astype(F32) + met_ref[i : i + 2, 128:192, :].astype(F32)
        out_ref[i : i + 2, 128:192, :] = dq_ref[i : i + 2]
        out_ref[i : i + 2, 192:256, :] = rope.astype(BF)
        lat = jnp.concatenate(
            [
                jnp.concatenate([ref[j, t * HALF : (t + 1) * HALF, :] for t in range(4)], axis=1)
                for j in (i, i + 1)
                for ref in (own_ref, oth_ref)
            ],
            axis=0,
        )
        total = total + dot(pair.reshape(256, 128).T.astype(BF), lat)
    out_ref[:, 256:288, :] = total.T.reshape(16, 32, 128).astype(BF)


def latent_kernel(r_ref, uk_ref, uv_ref, own_out, first_out, second_out, third_out, all_s):
    keys = jnp.concatenate([r_ref[i, 0:128, :] for i in range(0, 16, 2)], axis=1)
    values = jnp.concatenate(
        [jnp.concatenate([r_ref[i, 64:128, :], r_ref[i, 0:64, :]], axis=0) for i in range(1, 16, 2)], axis=1
    )
    all_s[:DL, :] = (dot_nt(uk_ref[...], keys) + dot_nt(uv_ref[...], values)).astype(BF)
    halves = [r_ref[c, 192:256, :].astype(F32) for c in range(2)]
    for i in range(2, 16):
        halves[i % 2] = halves[i % 2] + r_ref[i, 192:256, :].astype(F32)
    all_s[DL:, :] = jnp.concatenate(halves, axis=0).T[DR:, :].astype(BF)
    mine = lax.axis_index("head") // 4
    for k, out in enumerate((own_out, first_out, second_out, third_out)):
        out[...] = all_s[pl.ds(pl.multiple_of((mine ^ k) * PART, 16), PART), :]


def latent_terms(received, w_uk, w_uv):
    whole = pl.BlockSpec(memory_space=pltpu.VMEM)
    return pl.pallas_call(
        latent_kernel,
        in_specs=[whole] * 3,
        out_specs=[whole] * 4,
        out_shape=[jax.ShapeDtypeStruct((PART, TOK), BF)] * 4,
        scratch_shapes=[pltpu.VMEM((DL + DR, TOK), BF)],
        compiler_params=pltpu.CompilerParams(vmem_limit_bytes=16 << 20),
    )(received, w_uk, w_uv)


def four_kernel(a_ref, b_ref, c_ref, d_ref, out_ref):
    first = a_ref[...].astype(F32) + b_ref[...].astype(F32)
    out_ref[...] = (first + (c_ref[...].astype(F32) + d_ref[...].astype(F32))).astype(BF)


def place_kernel(a_ref, b_ref, c_ref, d_ref, out_ref):
    mine = lax.axis_index("head") // 4
    for k, ref in enumerate((a_ref, b_ref, c_ref, d_ref)):
        out_ref[pl.ds(pl.multiple_of((mine ^ k) * PART, 16), PART), :] = ref[...].astype(F32)


def unpack_kernel(r_ref, q_ref, uk_ref, uv_ref):
    low = low_lanes((HALF, TOK))
    for h in range(0, 8, 2):
        for c in range(2):
            rows = slice(c * HALF, c * HALF + HALF)
            i, j, at = 2 * h + c, 2 * h + 2 + c, h * 192
            q_ref[rows, at : at + 128] = r_ref[i, 128:192, :]
            first = r_ref[i, 192:256, :].astype(F32)
            second = pltpu.roll(r_ref[j, 192:256, :].astype(F32), DR, 1)
            turned = pltpu.roll(r_ref[j, 128:192, :].astype(F32), DR, 1)
            q_ref[rows, at + 128 : at + 256] = jnp.where(low, first, turned).astype(BF)
            q_ref[rows, at + 256 : at + 384] = jnp.where(low, turned, second).astype(BF)
    for i in range(16):
        ref = uv_ref if i % 2 else uk_ref
        ref[:, (i // 2) * 128 : (i // 2) * 128 + 128] = r_ref[i, 256:288, :].astype(F32)


def local(queries, latent, w_uk, w_uv, grad_out, positions, tool_result):
    every = [list(range(16))]
    swap = [(i, i ^ 1) for i in range(16)]

    def exchange(x):
        return lax.all_to_all(x, "ctx", 0, 0, tiled=True, axis_index_groups=every)

    def along_x(x, k):
        return lax.ppermute(x, "head", [(i, i ^ (4 * k)) for i in range(16)])

    def along_z(x, k):
        return lax.ppermute(x, "head", [(i, i ^ k) for i in range(16)])

    own = exchange(pack(queries, latent.T, grad_out, positions, tool_result))
    other = lax.ppermute(own, "ctx", swap)
    orders = own[:, 448, 0].astype(jnp.int32)
    mine = own_side(orders, own, w_uk, w_uv)
    keep, give, dq, rope = attend(orders, other, w_uk, w_uv, mine)
    met = lax.ppermute(give, "ctx", swap)
    (back,) = small(finish_kernel, (keep, met, rope, dq, own, other), [((16, BACK, 128), BF)])
    received = exchange(back)
    parts = latent_terms(received, w_uk, w_uv)
    (part,) = small(four_kernel, [parts[0]] + [along_x(parts[k], k) for k in (1, 2, 3)], [((PART, TOK), BF)])
    (part,) = small(four_kernel, [part] + [along_z(part, k) for k in (1, 2, 3)], [((PART, TOK), BF)])
    (whole,) = small(place_kernel, [part] + [along_x(part, k) for k in (1, 2, 3)], [((DL + DR, TOK), F32)])

    grad_queries, grad_w_uk, grad_w_uv = small(
        unpack_kernel, (received,), [((TOK, 1536), BF), ((32, 1024), F32), ((32, 1024), F32)]
    )
    return (grad_queries, whole.T, grad_w_uk, grad_w_uv)


def solution(mesh):
    placed = (
        P("ctx", "head"),
        P("ctx", None),
        P(None, "head"),
        P(None, "head"),
        P("ctx", "head"),
        P("ctx"),
        P("ctx"),
    )
    return jax.shard_map(
        local,
        mesh=mesh,
        in_specs=placed,
        out_specs=(P("ctx", "head"), P("ctx", None), P("ctx", "head"), P("ctx", "head")),
        check_vma=False,
    )
```

```python
import functools
import math

import jax
import jax.numpy as jnp
from jax import lax
from jax.experimental import pallas as pl
from jax.experimental.pallas import tpu as pltpu
from jax.sharding import PartitionSpec as P

DL = 512
DR = 64
DN = 128
DV = 128
TOK = 128
HALF = TOK // 2
ROWS = 464
BACK = 288
PART = (DL + DR) // 4
MASKED = -1e30
BF = jnp.bfloat16
F32 = jnp.float32


def dot(a, b):
    return lax.dot_general(a, b, (((1,), (0,)), ((), ())), preferred_element_type=F32)


def dot_nt(a, b):
    return lax.dot_general(a, b, (((1,), (1,)), ((), ())), preferred_element_type=F32)


def low_lanes(shape):
    return lax.broadcasted_iota(jnp.int32, shape, len(shape) - 1) < DR


def pack_kernel(q_hbm, lat_hbm, g_hbm, pos_hbm, tool_hbm, out_ref, q_ref, lat_ref, g_ref, pos_ref, tool_ref, sems):
    pairs = [(tool_hbm, tool_ref), (pos_hbm, pos_ref), (lat_hbm, lat_ref), (q_hbm, q_ref), (g_hbm, g_ref)]
    copies = [pltpu.make_async_copy(src, dst, sems.at[i]) for i, (src, dst) in enumerate(pairs)]
    for copy in copies:
        copy.start()
    for copy in copies[:3]:
        copy.wait()
    tokens = lat_ref[:DL, :].astype(F32).T.astype(BF)
    rope = jnp.concatenate([jnp.zeros((DR, TOK), F32), lat_ref[DL:, :].astype(F32)], axis=0).T
    keep = jnp.broadcast_to((1 - tool_ref[...]).astype(F32), (TOK, TOK)).T
    order = jnp.broadcast_to((pos_ref[...] // TOK).astype(F32), (16, TOK)).astype(BF)
    halves = [slice(c * HALF, c * HALF + HALF) for c in range(2)]
    for i in range(16):
        for t in range(4):
            out_ref[i, t * HALF : (t + 1) * HALF, :] = tokens[halves[i % 2], t * 128 : (t + 1) * 128]
        out_ref[i, 448:464, :] = order
    for copy in copies[3:]:
        copy.wait()
    low = low_lanes((TOK, TOK))
    for h in range(0, 8, 2):
        at = h * 192
        near = q_ref[:, at + 128 : at + 256].astype(F32)
        mid = pltpu.roll(near, DR, 1)
        end = pltpu.roll(q_ref[:, at + 256 : at + 384].astype(F32), DR, 1)
        nope = [q_ref[:, at : at + 128], jnp.where(low, mid, end).astype(BF)]
        ropes = [jnp.where(low, near, rope).astype(BF), jnp.where(low, end, rope).astype(BF)]
        for k in range(2):
            cotangent = (g_ref[:, (h + k) * 128 : (h + k) * 128 + 128].astype(F32) * keep).astype(BF)
            for c, rows in enumerate(halves):
                to = 2 * (h + k) + c
                out_ref[to, 256:320, :] = ropes[k][rows]
                out_ref[to, 320:384, :] = nope[k][rows]
                out_ref[to, 384:448, :] = cotangent[rows]


def pack(queries, lat_t, grad_out, positions, tool_result):
    return pl.pallas_call(
        pack_kernel,
        in_specs=[pl.BlockSpec(memory_space=pl.ANY)] * 5,
        out_specs=pl.BlockSpec(memory_space=pltpu.VMEM),
        out_shape=jax.ShapeDtypeStruct((16, ROWS, 128), BF),
        scratch_shapes=[
            pltpu.VMEM((TOK, 1536), BF),
            pltpu.VMEM((DL + DR, TOK), BF),
            pltpu.VMEM((TOK, 1024), BF),
            pltpu.VMEM((1, TOK), jnp.int32),
            pltpu.VMEM((1, TOK), jnp.int32),
            pltpu.SemaphoreType.DMA((5,)),
        ],
        compiler_params=pltpu.CompilerParams(vmem_limit_bytes=60 << 20),
    )(queries, lat_t, grad_out, positions.reshape(1, TOK), tool_result.reshape(1, TOK))


FACTOR = (DN + DR) ** -0.5 * math.log2(math.e)


def project(ref, source, weights, keys, values, ropes, turned):
    for b in range(4):
        rows = slice(b * 256, b * 256 + 256)
        four = [source[4 * b + k] for k in range(4)]
        tokens = jnp.concatenate(
            [jnp.concatenate([ref[i, t * HALF : (t + 1) * HALF, :] for t in range(4)], axis=1) for i in four], axis=0
        )
        both = dot(tokens, weights[...])
        rope = jnp.concatenate([ref[i, 256:320, :] for i in four], axis=0)
        key = both[:, 0:128].astype(BF)
        keys[rows, :] = key
        values[rows, :] = both[:, 128:256].astype(BF)
        ropes[rows, :] = rope
        turned[0:128, rows] = key.astype(F32).T.astype(BF)
        turned[128:256, rows] = rope.astype(F32).T.astype(BF)


def fetch_weights(uk_ref, uv_ref, weights, sems):
    columns = pl.ds(pl.multiple_of((lax.axis_index("ctx") // 2) * 128, 128), 128)
    copies = [
        pltpu.make_async_copy(ref.at[:, columns], weights.at[:, i * 128 : i * 128 + 128], sems.at[i])
        for i, ref in enumerate((uk_ref, uv_ref))
    ]
    for copy in copies:
        copy.start()
    return copies


def own_kernel(ord_ref, own_ref, uk_ref, uv_ref, qs, cs, keys, values, ropes, turned, s_out, g_out, top_out, total_out,
               mixed_out, weights, source, sems):
    copies = fetch_weights(uk_ref, uv_ref, weights, sems)
    for s in range(16):
        source[ord_ref[s]] = s
    low = low_lanes((HALF, TOK))
    for b in range(16):
        rows = slice(b * HALF, (b + 1) * HALF)
        rope = pltpu.roll(own_ref[source[b], 256:320, :].astype(F32), DR, 1)
        qs[rows, 0:128] = own_ref[source[b], 320:384, :]
        qs[rows, 128:256] = jnp.where(low, 0.0, rope).astype(BF)
        cs[rows, :] = own_ref[source[b], 384:448, :]
    for copy in copies:
        copy.wait()
    project(own_ref, source, weights, keys, values, ropes, turned)
    visible = lax.broadcasted_iota(jnp.int32, (256, 256), 0) <= lax.broadcasted_iota(jnp.int32, (256, 256), 1)
    for p in range(4):
        rows, first = slice(p * 256, p * 256 + 256), 128 * p * (p + 1)
        top = jnp.full((8, 256), MASKED, F32)
        for c in range(p + 1):
            at, to = slice(c * 256, c * 256 + 256), slice(first + c * 256, first + c * 256 + 256)
            sc = dot_nt(jnp.concatenate([keys[at, :], ropes[at, :]], axis=1), qs[rows, :]) * FACTOR
            if c == p:
                sc = jnp.where(visible, sc, MASKED)
            s_out[to, :] = sc
            g_out[to, :] = dot_nt(values[at, :], cs[rows, :])
            top = jnp.maximum(top, jnp.max(sc.reshape(32, 8, 256), axis=0))
        top = jnp.max(top, axis=0, keepdims=True)
        total = jnp.zeros((8, 256), F32)
        mixed = jnp.zeros((8, 256), F32)
        for c in range(p + 1):
            of = slice(first + c * 256, first + c * 256 + 256)
            e = jnp.exp2(s_out[of, :] - top)
            s_out[of, :] = e
            total = total + jnp.sum(e.reshape(32, 8, 256), axis=0)
            mixed = mixed + jnp.sum((e * g_out[of, :]).reshape(32, 8, 256), axis=0)
        top_out[p, :, :] = jnp.broadcast_to(top, (8, 256))
        total_out[p, :, :] = total
        mixed_out[p, :, :] = mixed


def own_side(orders, own, w_uk, w_uv):
    whole = pl.BlockSpec(memory_space=pltpu.VMEM)
    anywhere = pl.BlockSpec(memory_space=pl.ANY)
    shapes = [(1024, 256), (1024, 128), (1024, 128), (1024, 128), (1024, 128), (256, 1024)]
    return pl.pallas_call(
        own_kernel,
        in_specs=[pl.BlockSpec(memory_space=pltpu.SMEM), whole, anywhere, anywhere],
        out_specs=[whole] * 11,
        out_shape=[jax.ShapeDtypeStruct(shape, BF) for shape in shapes]
        + [jax.ShapeDtypeStruct(shape, F32) for shape in ((2560, 256), (2560, 256)) + ((4, 8, 256),) * 3],
        scratch_shapes=[pltpu.VMEM((DL, 256), BF), pltpu.SMEM((16,), jnp.int32), pltpu.SemaphoreType.DMA((2,))],
        compiler_params=pltpu.CompilerParams(vmem_limit_bytes=12 << 20),
    )(orders, own, w_uk, w_uv)


def attend_kernel(ord_ref, oth_ref, uk_ref, uv_ref, qs, cs, own_keys, own_values, own_ropes, own_turned, e_own, g_own,
                  top_own, total_own, mixed_own, keep_out, give_out, dq_out, rope_out,
                  weights, keys, values, ropes, turned, s_sc, g_sc, ds_sc, p_sc, kvg, dr, dqs, source, sems):
    scale = (DN + DR) ** -0.5
    core = lax.rem(lax.axis_index("ctx"), 2)
    copies = fetch_weights(uk_ref, uv_ref, weights, sems)
    for s in range(16):
        source[ord_ref[s]] = s
    for copy in copies:
        copy.wait()
    project(oth_ref, source, weights, keys, values, ropes, turned)
    row = lax.broadcasted_iota(jnp.int32, (256, 256), 0) // HALF
    lane = lax.broadcasted_iota(jnp.int32, (256, 256), 1) // HALF
    visible = row < lane + core
    spans = [slice(c * 256, (c + 1) * 256) for c in range(4)]

    def score(p, c):
        at = spans[c]
        sc = dot_nt(jnp.concatenate([keys[at, :], ropes[at, :]], axis=1), qs[spans[p], :]) * FACTOR
        if c == p:
            sc = jnp.where(visible, sc, MASKED)
        s_sc[p % 2, at, :] = sc
        g_sc[p % 2, at, :] = dot_nt(values[at, :], cs[spans[p], :])
        return jnp.max(sc.reshape(32, 8, 256), axis=0)

    tops = [score(0, 0)]
    for p in range(4):
        rows, first = spans[p], 128 * p * (p + 1)
        top = functools.reduce(jnp.maximum, tops, top_own[p])
        tops = []
        top = jnp.max(top, axis=0, keepdims=True)
        shrink = jnp.exp2(top_own[p] - top)
        total = total_own[p] * shrink
        mixed = mixed_own[p] * shrink
        for c in range(p + 1):
            at = spans[c]
            e = jnp.exp2(s_sc[p % 2, at, :] - top)
            s_sc[p % 2, at, :] = e
            total = total + jnp.sum(e.reshape(32, 8, 256), axis=0)
            mixed = mixed + jnp.sum((e * g_sc[p % 2, at, :]).reshape(32, 8, 256), axis=0)
            if p < 3:
                tops.append(score(p + 1, c))
        share = 1.0 / jnp.sum(total, axis=0, keepdims=True)
        delta = jnp.sum(mixed, axis=0, keepdims=True) * share
        own_share = shrink[0:1] * share
        if p < 3:
            tops.append(score(p + 1, p + 1))
        for c in range(p + 1):
            at, of = spans[c], slice(first + c * 256, first + c * 256 + 256)
            for side in range(2):
                prob = s_sc[p % 2, at, :] * share if side else e_own[of, :] * own_share
                g = g_sc[p % 2, at, :] if side else g_own[of, :]
                ds_sc[side, at, rows] = (prob * (g - delta)).astype(BF)
                p_sc[side, at, rows] = prob.astype(BF)
        upto = (p + 1) * 256
        dq = dot(own_turned[:, 0:upto], ds_sc[0, 0:upto, rows]) + dot(turned[:, 0:upto], ds_sc[1, 0:upto, rows])
        dqs[rows, :] = (dq * scale).T
    for c in range(4):
        at = spans[c]
        for side in range(2):
            key_part = dot(ds_sc[side, at, c * 256 :], qs[c * 256 :, :])
            kvg[0, side, at, :] = key_part[:, 0:128]
            dr[side, at, :] = key_part[:, 128:256]
            kvg[1, side, at, :] = dot(p_sc[side, at, c * 256 :], cs[c * 256 :, :])

    low = low_lanes((HALF, TOK))
    keep_scale = jnp.where(core == 0, scale, 1.0)
    give_scale = jnp.where(core == 0, 1.0, scale)
    for s in range(16):
        at = pl.ds(pl.multiple_of(ord_ref[s] * HALF, HALF), HALF)
        for side in range(2):
            half = slice(side * HALF, side * HALF + HALF)
            keep_out[s, half, :] = (kvg[core, side, at, :] * keep_scale).astype(BF)
            give_out[s, half, :] = (kvg[1 - core, 1 - side, at, :] * give_scale).astype(BF)
        give_out[s, 128:192, :] = (dr[1, at, :] * scale).astype(BF)
        dq_out[s, :, :] = dqs[at, 0:128].astype(BF)
        moved = pltpu.roll(dqs[at, 128:256], DR, 1)
        rope_out[s, :, :] = jnp.where(low, moved, dr[0, at, :] * scale).astype(BF)


def attend(orders, other, w_uk, w_uv, mine):
    whole = pl.BlockSpec(memory_space=pltpu.VMEM)
    anywhere = pl.BlockSpec(memory_space=pl.ANY)
    return pl.pallas_call(
        attend_kernel,
        in_specs=[pl.BlockSpec(memory_space=pltpu.SMEM), whole, anywhere, anywhere] + [whole] * 11,
        out_specs=[whole, whole, whole, whole],
        out_shape=[
            jax.ShapeDtypeStruct((16, TOK, 128), BF),
            jax.ShapeDtypeStruct((16, TOK + HALF, 128), BF),
            jax.ShapeDtypeStruct((16, HALF, 128), BF),
            jax.ShapeDtypeStruct((16, HALF, 128), BF),
        ],
        scratch_shapes=[
            pltpu.VMEM((DL, 256), BF),
            pltpu.VMEM((1024, 128), BF),
            pltpu.VMEM((1024, 128), BF),
            pltpu.VMEM((1024, 128), BF),
            pltpu.VMEM((256, 1024), BF),
            pltpu.VMEM((2, 1024, 256), F32),
            pltpu.VMEM((2, 1024, 256), F32),
            pltpu.VMEM((2, 1024, 1024), BF),
            pltpu.VMEM((2, 1024, 1024), BF),
            pltpu.VMEM((2, 2, 1024, 128), F32),
            pltpu.VMEM((2, 1024, 128), F32),
            pltpu.VMEM((1024, 256), F32),
            pltpu.SMEM((16,), jnp.int32),
            pltpu.SemaphoreType.DMA((2,)),
        ],
        compiler_params=pltpu.CompilerParams(vmem_limit_bytes=28 << 20),
    )(orders, other, w_uk, w_uv, *mine)


def small(kernel, inputs, outputs):
    whole = pl.BlockSpec(memory_space=pltpu.VMEM)
    return pl.pallas_call(
        kernel,
        in_specs=[whole] * len(inputs),
        out_specs=[whole] * len(outputs),
        out_shape=[jax.ShapeDtypeStruct(shape, dtype) for shape, dtype in outputs],
        compiler_params=pltpu.CompilerParams(vmem_limit_bytes=16 << 20),
    )(*inputs)


def share_kernel(own_ref, out_ref):
    out_ref[...] = own_ref[:, 0:320, :]


def finish_kernel(keep_ref, met_ref, rope_ref, dq_ref, own_ref, oth_ref, out_ref):
    total = jnp.zeros((128, DL), F32)
    for i in range(0, 16, 2):
        pair = keep_ref[i : i + 2].astype(F32) + met_ref[i : i + 2, 0:128, :].astype(F32)
        out_ref[i : i + 2, 0:128, :] = pair.astype(BF)
        rope = rope_ref[i : i + 2].astype(F32) + met_ref[i : i + 2, 128:192, :].astype(F32)
        out_ref[i : i + 2, 128:192, :] = dq_ref[i : i + 2]
        out_ref[i : i + 2, 192:256, :] = rope.astype(BF)
        lat = jnp.concatenate(
            [
                jnp.concatenate([ref[j, t * HALF : (t + 1) * HALF, :] for t in range(4)], axis=1)
                for j in (i, i + 1)
                for ref in (own_ref, oth_ref)
            ],
            axis=0,
        )
        total = total + dot(pair.reshape(256, 128).T.astype(BF), lat)
    out_ref[:, 256:288, :] = total.T.reshape(16, 32, 128).astype(BF)


def latent_kernel(r_ref, uk_ref, uv_ref, own_out, first_out, second_out, third_out, all_s):
    keys = jnp.concatenate([r_ref[i, 0:128, :] for i in range(0, 16, 2)], axis=1)
    values = jnp.concatenate(
        [jnp.concatenate([r_ref[i, 64:128, :], r_ref[i, 0:64, :]], axis=0) for i in range(1, 16, 2)], axis=1
    )
    all_s[:DL, :] = (dot_nt(uk_ref[...], keys) + dot_nt(uv_ref[...], values)).astype(BF)
    halves = [r_ref[c, 192:256, :].astype(F32) for c in range(2)]
    for i in range(2, 16):
        halves[i % 2] = halves[i % 2] + r_ref[i, 192:256, :].astype(F32)
    all_s[DL:, :] = jnp.concatenate(halves, axis=0).T[DR:, :].astype(BF)
    mine = lax.axis_index("head") // 4
    for k, out in enumerate((own_out, first_out, second_out, third_out)):
        out[...] = all_s[pl.ds(pl.multiple_of((mine ^ k) * PART, 16), PART), :]


def latent_terms(received, w_uk, w_uv):
    whole = pl.BlockSpec(memory_space=pltpu.VMEM)
    return pl.pallas_call(
        latent_kernel,
        in_specs=[whole] * 3,
        out_specs=[whole] * 4,
        out_shape=[jax.ShapeDtypeStruct((PART, TOK), BF)] * 4,
        scratch_shapes=[pltpu.VMEM((DL + DR, TOK), BF)],
        compiler_params=pltpu.CompilerParams(vmem_limit_bytes=16 << 20),
    )(received, w_uk, w_uv)


def four_kernel(a_ref, b_ref, c_ref, d_ref, out_ref):
    first = a_ref[...].astype(F32) + b_ref[...].astype(F32)
    out_ref[...] = (first + (c_ref[...].astype(F32) + d_ref[...].astype(F32))).astype(BF)


def place_kernel(a_ref, b_ref, c_ref, d_ref, out_ref):
    mine = lax.axis_index("head") // 4
    for k, ref in enumerate((a_ref, b_ref, c_ref, d_ref)):
        out_ref[pl.ds(pl.multiple_of((mine ^ k) * PART, 16), PART), :] = ref[...].astype(F32)


def unpack_kernel(r_ref, q_ref, uk_ref, uv_ref):
    low = low_lanes((HALF, TOK))
    for h in range(0, 8, 2):
        for c in range(2):
            rows = slice(c * HALF, c * HALF + HALF)
            i, j, at = 2 * h + c, 2 * h + 2 + c, h * 192
            q_ref[rows, at : at + 128] = r_ref[i, 128:192, :]
            first = r_ref[i, 192:256, :].astype(F32)
            second = pltpu.roll(r_ref[j, 192:256, :].astype(F32), DR, 1)
            turned = pltpu.roll(r_ref[j, 128:192, :].astype(F32), DR, 1)
            q_ref[rows, at + 128 : at + 256] = jnp.where(low, first, turned).astype(BF)
            q_ref[rows, at + 256 : at + 384] = jnp.where(low, turned, second).astype(BF)
    for i in range(16):
        ref = uv_ref if i % 2 else uk_ref
        ref[:, (i // 2) * 128 : (i // 2) * 128 + 128] = r_ref[i, 256:288, :].astype(F32)


def local(queries, latent, w_uk, w_uv, grad_out, positions, tool_result):
    every = [list(range(16))]
    swap = [(i, i ^ 1) for i in range(16)]

    def exchange(x):
        return lax.all_to_all(x, "ctx", 0, 0, tiled=True, axis_index_groups=every)

    def along_x(x, k):
        return lax.ppermute(x, "head", [(i, i ^ (4 * k)) for i in range(16)])

    def along_z(x, k):
        return lax.ppermute(x, "head", [(i, i ^ k) for i in range(16)])

    own = exchange(pack(queries, latent.T, grad_out, positions, tool_result))
    (shared,) = small(share_kernel, (own,), [((16, 320, 128), BF)])
    other = lax.ppermute(shared, "ctx", swap)
    orders = own[:, 448, 0].astype(jnp.int32)
    mine = own_side(orders, own, w_uk, w_uv)
    keep, give, dq, rope = attend(orders, other, w_uk, w_uv, mine)
    met = lax.ppermute(give, "ctx", swap)
    (back,) = small(finish_kernel, (keep, met, rope, dq, own, other), [((16, BACK, 128), BF)])
    received = exchange(back)
    parts = latent_terms(received, w_uk, w_uv)
    (part,) = small(four_kernel, [parts[0]] + [along_x(parts[k], k) for k in (1, 2, 3)], [((PART, TOK), BF)])
    (part,) = small(four_kernel, [part] + [along_z(part, k) for k in (1, 2, 3)], [((PART, TOK), BF)])
    (whole,) = small(place_kernel, [part] + [along_x(part, k) for k in (1, 2, 3)], [((DL + DR, TOK), F32)])

    grad_queries, grad_w_uk, grad_w_uv = small(
        unpack_kernel, (received,), [((TOK, 1536), BF), ((32, 1024), F32), ((32, 1024), F32)]
    )
    return (grad_queries, whole.T, grad_w_uk, grad_w_uv)


def solution(mesh):
    placed = (
        P("ctx", "head"),
        P("ctx", None),
        P(None, "head"),
        P(None, "head"),
        P("ctx", "head"),
        P("ctx"),
        P("ctx"),
    )
    return jax.shard_map(
        local,
        mesh=mesh,
        in_specs=placed,
        out_specs=(P("ctx", "head"), P("ctx", None), P("ctx", "head"), P("ctx", "head")),
        check_vma=False,
    )
```
